256 devices in a mesh: replica: 8 (over x, y_lo), tensor: 32 (over z, y_hi, core).
Axes of the slice: x: 4, y: 4 (y_hi: 2, y_lo: 2; y = y_hi * 2 + y_lo), z: 8, core: 2. Of those that a mesh axis runs over, the one named last changes fastest.
Arguments:
- inputs: bfloat16 [8, 1280, 2304], P('replica', 'tensor'), may hold values from -6 to 6
- cotangent: bfloat16 [8, 1280, 2304], P('replica', 'tensor'), may hold values from -6 to 6
- gate_weight: bfloat16 [8, 2304, 9216], P('replica', None, 'tensor'), may hold values from -6 to 6
- up_weight: bfloat16 [8, 2304, 9216], P('replica', None, 'tensor'), may hold values from -6 to 6
- down_weight: bfloat16 [8, 9216, 2304], P('replica', 'tensor'), may hold values from -6 to 6
- step: int32 [1], replicated, may hold values from 0 to 2999
Outputs:
- input_grad: bfloat16 [8, 1280, 2304], P('replica', 'tensor')
- gate_next: bfloat16 [8, 2304, 9216], P('replica', None, 'tensor')
- up_next: bfloat16 [8, 2304, 9216], P('replica', None, 'tensor')
- down_next: bfloat16 [8, 9216, 2304], P('replica', 'tensor')
The draws below stay inside these ranges and needn't reach their ends.
All inputs are finite; a program needn't handle non-finite values.
Results may differ from the reference program's by a relative error of at most 0.0052.
Values may be sent and summed in bfloat16 or wider, within the bound.
A program may use at most 128 MiB of HBM per device.

```python
import math
import jax
import jax.numpy as jnp
from jax import lax

D = 2304
FF = 9216
TOKENS = 1280
REPLICAS = 8
N_REPLICA = 8


def levels(stream_key, extent, shards, least, largest):
    def one(position, shards_of):
        heights = jax.random.uniform(jax.random.fold_in(jax.random.fold_in(stream_key, 6), position), (shards_of,), jnp.float32, least / len(shards), largest / len(shards))
        return jnp.repeat(jnp.exp(heights), extent[position] // shards_of).reshape((-1,) + (1,) * (len(extent) - position - 1))

    level = one(*shards[0])
    for cut in shards[1:]:
        level = level * one(*cut)
    return level


def scatter_about(stream_key, dims, width, most, cuts=(), kind=jnp.bfloat16):
    level = levels(stream_key, dims, cuts, -0.22, 0.18) if cuts else 1.0
    drawn = jax.random.normal(stream_key, dims, jnp.float32) * width * level
    return jnp.minimum(jnp.maximum(drawn, -most), most).astype(kind)


def setup_inputs(seed: int = 0) -> dict:
    splits = jax.random.split(jax.random.key(seed), 7)
    inputs = scatter_about(splits[0], (REPLICAS, TOKENS, D), 1.0, 6.0, ((0, 8), (1, 32)))
    cotangent = scatter_about(splits[1], (REPLICAS, TOKENS, D), 1.0, 6.0, ((0, 8), (1, 32)))
    gate_weight = scatter_about(splits[2], (REPLICAS, D, FF), 1.0, 6.0, ((0, 8), (2, 32)))
    up_weight = scatter_about(splits[3], (REPLICAS, D, FF), 1.0, 6.0, ((0, 8), (2, 32)))
    down_weight = scatter_about(splits[4], (REPLICAS, FF, D), 1.0, 6.0, ((0, 8), (1, 32)))
    step = jax.random.randint(splits[5], (1,), 0, 3000).astype(jnp.int32)
    return dict(inputs=inputs, cotangent=cotangent, gate_weight=gate_weight, up_weight=up_weight, down_weight=down_weight, step=step)


gelu_c = 0.7978845608028654
gelu_k = 0.044715
learn_rate = 1.0

def gelu_parts(value):
    inner = gelu_c * (value + gelu_k * value * value * value)
    tangent = jnp.tanh(inner)
    act = 0.5 * value * (1.0 + tangent)
    slope = 0.5 * (1.0 + tangent) + 0.5 * value * (1.0 - tangent * tangent) * gelu_c * (1.0 + 3.0 * gelu_k * value * value)
    return (act, slope)

def train_one(operands):
    rows, out_grad, w_gate, w_up, w_down = operands
    scale_model = 1.0 / math.sqrt(D)
    scale_hidden = 1.0 / math.sqrt(FF)
    gate = jnp.dot(rows, w_gate, preferred_element_type=jnp.float32) * scale_model
    up = jnp.dot(rows, w_up, preferred_element_type=jnp.float32) * scale_model
    act, slope = gelu_parts(gate)
    hidden = (act * up).astype(jnp.bfloat16)
    hidden_grad = lax.dot_general(out_grad, w_down, (((1,), (1,)), ((), ())), preferred_element_type=jnp.float32) * scale_hidden
    gate_grad = (hidden_grad * up * slope).astype(jnp.bfloat16)
    up_grad = (hidden_grad * act).astype(jnp.bfloat16)
    back = lax.dot_general(gate_grad, w_gate, (((1,), (1,)), ((), ())), preferred_element_type=jnp.float32)
    back = back + lax.dot_general(up_grad, w_up, (((1,), (1,)), ((), ())), preferred_element_type=jnp.float32)
    input_grad = (back * scale_model).astype(jnp.bfloat16)
    wgrad_gate = lax.dot_general(rows, gate_grad, (((0,), (0,)), ((), ())), preferred_element_type=jnp.float32) * scale_model
    wgrad_up = lax.dot_general(rows, up_grad, (((0,), (0,)), ((), ())), preferred_element_type=jnp.float32) * scale_model
    wgrad_down = lax.dot_general(hidden, out_grad, (((0,), (0,)), ((), ())), preferred_element_type=jnp.float32) * scale_hidden
    new_gate = (w_gate.astype(jnp.float32) - learn_rate * wgrad_gate).astype(jnp.bfloat16)
    new_up = (w_up.astype(jnp.float32) - learn_rate * wgrad_up).astype(jnp.bfloat16)
    new_down = (w_down.astype(jnp.float32) - learn_rate * wgrad_down).astype(jnp.bfloat16)
    return (input_grad, new_gate, new_up, new_down)

def average_peer(tensor, peers):
    other = jnp.take(tensor, peers, axis=0)
    return ((tensor.astype(jnp.float32) + other.astype(jnp.float32)) * 0.5).astype(jnp.bfloat16)

def reference(inputs, cotangent, gate_weight, up_weight, down_weight, step):
    input_grad, new_gate, new_up, new_down = lax.map(train_one, (inputs, cotangent, gate_weight, up_weight, down_weight))
    distance = jnp.left_shift(jnp.int32(1), (step[0] % 3).astype(jnp.int32))
    peers = ((jnp.arange(N_REPLICA, dtype=jnp.int32) + distance) % N_REPLICA).astype(jnp.int32)
    return (input_grad, average_peer(new_gate, peers), average_peer(new_up, peers), average_peer(new_down, peers))
```

```python
import functools
import math

import jax
import jax.numpy as jnp
from jax import lax
from jax.experimental import pallas as pl
from jax.experimental.pallas import tpu as pltpu
from jax.sharding import PartitionSpec as P

D = 2304
FF = 9216
TOKENS = 1280
UNITS = 288
WIDE = 384
BLOCK = 80
HALF = D // 2
PIECE = 256
PIECES = D // PIECE
PACK = 3 * UNITS

gelu_c = 0.7978845608028654
gelu_k = 0.044715
learn_rate = 1.0
scale_model = 1.0 / math.sqrt(D)
scale_hidden = 1.0 / math.sqrt(FF)

MESH = pl.DeviceIdType.MESH
F32 = jnp.float32
BF16 = jnp.bfloat16

PLACE = {0: 0, -1: 1, 1: 2, -2: 3, 2: 4, -3: 5, 3: 6, 4: 7, -4: 7}


def block_rows(offset, pair):
    return pl.ds(BLOCK * (2 * PLACE[offset] + pair), BLOCK)


def gelu_parts(value):
    inner = gelu_c * (value + gelu_k * value * value * value)
    tangent = jnp.tanh(inner)
    act = 0.5 * value * (1.0 + tangent)
    slope = 0.5 * (1.0 + tangent) + 0.5 * value * (1.0 - tangent * tangent) * gelu_c * (
        1.0 + 3.0 * gelu_k * value * value
    )
    return act, slope


def dot(left, right, dims):
    return lax.dot_general(left, right, (dims, ((), ())), preferred_element_type=F32)


def kernel(
    distance,
    x_in, cot_in, wg_in, wu_in, wd_in,
    grad_out, gate_out, up_out, down_out,
    xs, cs, wgu, wd, gu, hid, gate_up, part, part_sib, chain, new_buf, peer_buf,
    raw_gate, raw_up, raw_down, wide32, pair32, ysend, ybuf, fin, rows32,
    load_sem, pair_ss, pair_rs, zx_ss, zx_rs, zc_ss, zc_rs, yx_ss, yx_rs, yc_ss, yc_rs,
    sx_ss, sx_rs, sc_ss, sc_rs, p_ss, p_rs, ch_ss, ch_rs, ys_ss, ys_rs, f_ss, f_rs,
    g_ss, g_rs, out_sem,
):
    r = lax.axis_index("replica")
    t = lax.axis_index("tensor")
    z, yh, c = t // 4, (t // 2) % 2, t % 2
    base = yh * 2 + c
    ahead = (r, lax.rem(z + 1, 8) * 4 + base)
    behind = (r, lax.rem(z + 7, 8) * 4 + base)
    across = (r, z * 4 + (1 - yh) * 2 + c)
    sibling = (r, z * 4 + yh * 2 + (1 - c))
    gives_to = (lax.rem(r + 8 - distance, 8), t)
    takes_from = (lax.rem(r + distance, 8), t)

    mine = pl.ds(pl.multiple_of(c * HALF, 128), HALF)
    other = pl.ds(pl.multiple_of((1 - c) * HALF, 128), HALF)

    def remote(src, dst, ss, rs, device):
        return pltpu.make_async_remote_copy(
            src_ref=src, dst_ref=dst, send_sem=ss, recv_sem=rs, device_id=device, device_id_type=MESH
        )

    loads = [
        pltpu.make_async_copy(wg_in.at[0], raw_gate, load_sem.at[0]),
        pltpu.make_async_copy(wu_in.at[0], raw_up, load_sem.at[1]),
        pltpu.make_async_copy(wd_in.at[0], wd.at[pl.ds(0, UNITS), :], load_sem.at[2]),
    ]
    for load in loads:
        load.start()

    barrier = pltpu.get_barrier_semaphore()
    for device in (ahead, behind, across, sibling, takes_from):
        pl.semaphore_signal(barrier, inc=1, device_id=device, device_id_type=MESH)
    wide32[0] = x_in[0].astype(F32)
    wide32[1] = cot_in[0].astype(F32)
    pl.semaphore_wait(barrier, 5)

    started = []

    def begin(copy):
        copy.start()
        started.append(copy)
        return copy

    forty = pl.ds(pl.multiple_of(c * 40, 8), 40)
    pairs = [
        begin(remote(wide32.at[a, :, other], pair32.at[a, forty, :], pair_ss.at[a], pair_rs.at[a], sibling))
        for a in range(2)
    ]
    for a in range(2):
        pair32[a, forty, :] = wide32[a, :, mine]

    def x_hop(sign, k):
        index = PLACE[sign * k]
        return remote(
            xs.at[block_rows(-sign * (k - 1), 0), mine], xs.at[block_rows(-sign * k, 0), mine],
            zx_ss.at[PLACE[-sign * k] if k < 4 else 7], zx_rs.at[PLACE[-sign * k]], ahead if sign > 0 else behind,
        )

    def c_hop(sign, k, pair):
        slot = 2 * PLACE[-sign * k] + pair
        return remote(
            cs.at[block_rows(-sign * (k - 1), pair), mine], cs.at[block_rows(-sign * k, pair), mine],
            zc_ss.at[slot], zc_rs.at[slot], ahead if sign > 0 else behind,
        )

    def x_across(offset):
        i = PLACE[offset]
        return remote(
            xs.at[block_rows(offset, 0), mine], xs.at[block_rows(offset, 1), mine], yx_ss.at[i], yx_rs.at[i], across
        )

    def to_sibling(buf, place, ss, rs):
        at = buf.at[pl.ds(160 * place, 160), mine]
        return remote(at, at, ss.at[place], rs.at[place], sibling)

    pairs[0].wait_recv()
    xs[block_rows(0, 0), mine] = pair32[0].astype(BF16)
    x_fly = {}
    for sign in (1, -1):
        x_fly[sign] = begin(x_hop(sign, 1))
    y_fly = {0: begin(x_across(0))}
    pairs[1].wait_recv()
    cs[block_rows(0, 0), mine] = pair32[1].astype(BF16)
    c_pair = begin(
        remote(cs.at[block_rows(0, 0), mine], cs.at[block_rows(0, 1), mine], yc_ss, yc_rs, across)
    )
    c_fly = {}
    for sign in (1, -1):
        c_fly[sign, 0] = begin(c_hop(sign, 1, 0))

    zeros = jnp.zeros((D, 128), BF16)
    wgu[:, pl.ds(256, 128)] = zeros
    wgu[:, pl.ds(640, 128)] = zeros
    wd[pl.ds(UNITS, WIDE - UNITS), :] = jnp.zeros((WIDE - UNITS, D), BF16)
    for i, raw in enumerate((raw_gate, raw_up)):
        loads[i].wait()
        wgu[:, pl.ds(WIDE * i, 256)] = raw[:, pl.ds(0, 256)]
        wgu[:, pl.ds(WIDE * i + 256, 32)] = raw[:, pl.ds(256, 32)]
    loads[2].wait()

    c_pair.wait_recv()
    for sign in (1, -1):
        c_fly[sign, 1] = begin(c_hop(sign, 1, 1))
    sib_fly = {(1, 0): begin(to_sibling(cs, 0, sc_ss, sc_rs))}
    y_fly[0].wait_recv()
    sib_fly[0, 0] = begin(to_sibling(xs, 0, sx_ss, sx_rs))

    def forward_a(row, count):
        rows = pl.ds(row, count)
        gate_up[pl.ds(0, count), :] = dot(xs[rows, :], wgu[...], ((1,), (0,)))

    def forward_b(row, count):
        rows = pl.ds(row, count)
        hidden_grad = dot(cs[rows, :], wd[...], ((1,), (1,))) * scale_hidden
        gate = gate_up[pl.ds(0, count), pl.ds(0, WIDE)] * scale_model
        up = gate_up[pl.ds(0, count), pl.ds(WIDE, WIDE)] * scale_model
        act, slope = gelu_parts(gate)
        hid[rows, :] = (act * up).astype(BF16)
        gu[rows, pl.ds(0, WIDE)] = (hidden_grad * up * slope).astype(BF16)
        gu[rows, pl.ds(WIDE, WIDE)] = (hidden_grad * act).astype(BF16)

    def backward(row, count):
        rows = pl.ds(row, count)
        for j in range(3):
            cols = pl.ds(768 * j, 768)
            part[rows, cols] = dot(gu[rows, :], wgu[cols, :], ((1,), (1,)))

    def part_to_sibling(row, count, index):
        rows = pl.ds(row, count)
        return remote(part.at[rows, other], part_sib.at[rows, :], p_ss.at[index], p_rs.at[index], sibling)

    part_fly = {}
    chunk_of = lambda k: (0, 160) if k == 0 else ((1120, 160) if k == 4 else (160 + 320 * (k - 1), 320))

    for k in range(1, 5):
        row, count = chunk_of(k - 1)
        x_signs = (1, -1) if k < 4 else (1,)
        for sign in x_signs:
            x_fly[sign].wait_recv()
            if k < 3 or (k == 3 and sign > 0):
                x_fly[sign] = begin(x_hop(sign, k + 1))
            y_fly[-sign * k] = begin(x_across(-sign * k))
        for place in ((0,) if k == 1 else (2 * k - 3, 2 * k - 2)):
            sib_fly[0, place].wait_recv()
            sib_fly[1, place].wait_recv()
        forward_a(row, count)
        for pair in (0, 1):
            for sign in ((1, -1) if k < 4 else ((1,) if pair == 0 else (-1,))):
                c_fly[sign, pair].wait_recv()
                if k < 3 or (k == 3 and (sign > 0) == (pair == 0)):
                    c_fly[sign, pair] = begin(c_hop(sign, k + 1, pair))
            if pair == 0:
                forward_b(row, count)
        places = (2 * k - 1, 2 * k) if k < 4 else (7,)
        offsets = (-k, k) if k < 4 else (-4,)
        for place in places:
            sib_fly[1, place] = begin(to_sibling(cs, place, sc_ss, sc_rs))
        for place, offset in zip(places, offsets):
            y_fly[offset].wait_recv()
            sib_fly[0, place] = begin(to_sibling(xs, place, sx_ss, sx_rs))
        if k < 4:
            backward(row, count)
            part_fly[k - 1] = begin(part_to_sibling(row, count, k - 1))

    sib_fly[0, 7].wait_recv()
    sib_fly[1, 7].wait_recv()
    row, count = chunk_of(4)
    forward_a(row, count)
    forward_b(row, count)

    def gossip(j):
        return remote(new_buf.at[j], peer_buf.at[j], g_ss.at[j], g_rs.at[j], gives_to)

    def update(j):
        cols = pl.ds(pl.multiple_of(j * PIECE, PIECE), PIECE)
        sums = dot(xs[:, cols], gu[...], ((0,), (0,)))
        fresh = wgu[cols, :].astype(F32) - learn_rate * (sums * scale_model)
        for i in range(2):
            new_buf[j, pl.ds(PIECE * i, PIECE), :] = fresh[:, WIDE * i : WIDE * i + 256].astype(BF16)
            packed = fresh[0:64, WIDE * i + 256 : WIDE * i + 384]
            for q in range(1, 4):
                packed = packed + pltpu.roll(fresh[64 * q : 64 * q + 64, WIDE * i + 256 : WIDE * i + 384], 32 * q, 1)
            new_buf[j, pl.ds(2 * PIECE, 64), pl.ds(128 * i, 128)] = packed.astype(BF16)
        down = dot(hid[...], cs[:, cols], ((0,), (0,)))
        fresh_down = wd[pl.ds(0, UNITS), cols].astype(F32) - learn_rate * (down[0:UNITS] * scale_hidden)
        new_buf[j, pl.ds(2 * UNITS, UNITS), :] = fresh_down.astype(BF16)
        gossip(j).start()

    def update_step(j, carry):
        update(j)
        return carry

    lax.fori_loop(0, 2, update_step, 0)
    backward(row, count)
    part_fly[4] = begin(part_to_sibling(row, count, 4))
    part_fly[3] = None

    row, count = chunk_of(3)
    backward(row, count)
    part_fly[3] = begin(part_to_sibling(row, count, 3))
    for i in range(5):
        part_fly[i].wait_recv()

    def share(offset, pair):
        rows = block_rows(offset, pair)
        return part[rows, mine] + part_sib[rows, :]

    chains = [(1, 0, (4, 3, 2, 1)), (1, 1, (3, 2, 1)), (-1, 0, (-3, -2, -1)), (-1, 1, (-4, -3, -2, -1))]
    slot_of = {}
    for n, (_, _, stops) in enumerate(chains):
        for m in range(len(stops)):
            slot_of[n, m] = len(slot_of)

    def chain_hop(n, m, src):
        slot = slot_of[n, m]
        return remote(src, chain.at[slot], ch_ss.at[slot], ch_rs.at[slot], ahead if chains[n][0] > 0 else behind)

    chain_fly = {}
    for n, (_, pair, stops) in enumerate(chains):
        rows = block_rows(stops[0], pair)
        part[rows, mine] = share(stops[0], pair)
        chain_fly[n] = begin(chain_hop(n, 0, part.at[rows, mine]))

    lax.fori_loop(2, PIECES, update_step, 0)

    for m in range(1, 4):
        for n, (_, pair, stops) in enumerate(chains):
            if m < len(stops):
                slot = slot_of[n, m - 1]
                chain_fly[n].wait_recv()
                chain[slot] = chain[slot] + share(stops[m], pair)
                chain_fly[n] = begin(chain_hop(n, m, chain.at[slot]))
    last = [slot_of[n, len(chains[n][2]) - 1] for n in range(4)]
    for n in (1, 3):
        chain_fly[n].wait_recv()
    ysend[...] = share(0, 1) + chain[last[1]] + chain[last[3]]
    y_sum = begin(remote(ysend, ybuf, ys_ss, ys_rs, across))
    for n in (0, 2):
        chain_fly[n].wait_recv()
    total = share(0, 0) + chain[last[0]] + chain[last[2]]
    y_sum.wait_recv()
    fin[...] = (total + ybuf[...]) * scale_model
    theirs = pl.ds(pl.multiple_of((1 - c) * 40, 8), 40)
    rows_fly = begin(remote(fin.at[theirs, :], rows32.at[:, mine], f_ss, f_rs, sibling))
    rows32[:, mine] = fin[forty, :]
    rows_fly.wait_recv()
    grad_out[0] = rows32[...].astype(BF16)

    def outs(j):
        cols = pl.ds(pl.multiple_of(j * PIECE, PIECE), PIECE)
        return [
            pltpu.make_async_copy(raw_gate.at[cols, :], gate_out.at[0, cols, :], out_sem.at[0, j]),
            pltpu.make_async_copy(raw_up.at[cols, :], up_out.at[0, cols, :], out_sem.at[1, j]),
            pltpu.make_async_copy(raw_down.at[:, cols], down_out.at[0, :, cols], out_sem.at[2, j]),
        ]

    def mean_step(j, carry):
        gossip(j).wait_recv()
        first = pl.multiple_of(j * PIECE, PIECE)
        cols = pl.ds(first, PIECE)
        for i, raw in enumerate((raw_gate, raw_up)):
            at = pl.ds(PIECE * i, PIECE)
            mean = (new_buf[j, at, :].astype(F32) + peer_buf[j, at, :].astype(F32)) * 0.5
            raw[cols, pl.ds(0, 256)] = mean.astype(BF16)
            at, lanes = pl.ds(2 * PIECE, 64), pl.ds(128 * i, 128)
            mean = (new_buf[j, at, lanes].astype(F32) + peer_buf[j, at, lanes].astype(F32)) * 0.5
            for q in range(4):
                turned = mean if q == 0 else pltpu.roll(mean, 128 - 32 * q, 1)
                raw[pl.ds(pl.multiple_of(first + 64 * q, 64), 64), pl.ds(256, 32)] = turned[:, 0:32].astype(BF16)
        at = pl.ds(2 * UNITS, UNITS)
        mean = (new_buf[j, at, :].astype(F32) + peer_buf[j, at, :].astype(F32)) * 0.5
        raw_down[:, cols] = mean.astype(BF16)
        for copy in outs(j):
            copy.start()
        return carry

    lax.fori_loop(0, PIECES, mean_step, 0)

    for copy in started:
        copy.wait_send()

    def finish(j, carry):
        gossip(j).wait_send()
        for copy in outs(j):
            copy.wait()
        return carry

    lax.fori_loop(0, PIECES, finish, 0)


def call(distance, arrays):
    dma = pltpu.SemaphoreType.DMA
    vmem = pl.BlockSpec(memory_space=pltpu.VMEM)
    hbm = pl.BlockSpec(memory_space=pl.ANY)
    return pl.pallas_call(
        functools.partial(kernel, distance),
        out_shape=(
            jax.ShapeDtypeStruct((1, 40, D), BF16),
            jax.ShapeDtypeStruct((1, D, UNITS), BF16),
            jax.ShapeDtypeStruct((1, D, UNITS), BF16),
            jax.ShapeDtypeStruct((1, UNITS, D), BF16),
        ),
        in_specs=[vmem, vmem, hbm, hbm, hbm],
        out_specs=(vmem, hbm, hbm, hbm),
        scratch_shapes=[
            pltpu.VMEM((TOKENS, D), BF16),
            pltpu.VMEM((TOKENS, D), BF16),
            pltpu.VMEM((D, 2 * WIDE), BF16),
            pltpu.VMEM((WIDE, D), BF16),
            pltpu.VMEM((TOKENS, 2 * WIDE), BF16),
            pltpu.VMEM((TOKENS, WIDE), BF16),
            pltpu.VMEM((320, 2 * WIDE), F32),
            pltpu.VMEM((TOKENS, D), F32),
            pltpu.VMEM((TOKENS, HALF), F32),
            pltpu.VMEM((14, BLOCK, HALF), F32),
            pltpu.VMEM((PIECES, PACK, PIECE), BF16),
            pltpu.VMEM((PIECES, PACK, PIECE), BF16),
            pltpu.VMEM((D, UNITS), BF16),
            pltpu.VMEM((D, UNITS), BF16),
            pltpu.VMEM((UNITS, D), BF16),
            pltpu.VMEM((2, 40, D), F32),
            pltpu.VMEM((2, BLOCK, HALF), F32),
            pltpu.VMEM((BLOCK, HALF), F32),
            pltpu.VMEM((BLOCK, HALF), F32),
            pltpu.VMEM((BLOCK, HALF), F32),
            pltpu.VMEM((40, D), F32),
            dma((3,)), dma((2,)), dma((2,)),
            dma((8,)), dma((8,)), dma((16,)), dma((16,)), dma((8,)), dma((8,)), dma, dma,
            dma((8,)), dma((8,)), dma((8,)), dma((8,)), dma((5,)), dma((5,)), dma((14,)), dma((14,)),
            dma, dma, dma, dma,
            dma((PIECES,)), dma((PIECES,)), dma((3, PIECES)),
        ],
        compiler_params=pltpu.CompilerParams(
            collective_id=distance, has_side_effects=True, vmem_limit_bytes=63 * 2**20
        ),
        cost_estimate=pl.CostEstimate(flops=13600000000, bytes_accessed=10000000, transcendentals=400000),
        name=f"gossip_by_{distance}",
    )(*arrays)


def body(inputs, cotangent, gate_weight, up_weight, down_weight, step):
    arrays = (inputs, cotangent, gate_weight, up_weight, down_weight)
    branches = [functools.partial(call, 1 << power) for power in range(3)]
    return lax.switch(step[0] % 3, branches, arrays)


def solution(mesh):
    in_specs = (
        P("replica", "tensor", None),
        P("replica", "tensor", None),
        P("replica", None, "tensor"),
        P("replica", None, "tensor"),
        P("replica", "tensor", None),
        P(),
    )
    out_specs = (
        P("replica", "tensor", None),
        P("replica", None, "tensor"),
        P("replica", None, "tensor"),
        P("replica", "tensor", None),
    )
    return jax.shard_map(body, mesh=mesh, in_specs=in_specs, out_specs=out_specs, check_vma=False)
```

```python
import functools
import math

import jax
import jax.numpy as jnp
from jax import lax
from jax.experimental import pallas as pl
from jax.experimental.pallas import tpu as pltpu
from jax.sharding import PartitionSpec as P

D = 2304
FF = 9216
TOKENS = 1280
UNITS = 288
WIDE = 384
BLOCK = 80
PAIR = 160
HALF = D // 2
PIECE = 256
PIECES = D // PIECE
EARLY = 4
LONG = 2

gelu_c = 0.7978845608028654
gelu_k = 0.044715
learn_rate = 1.0
scale_model = 1.0 / math.sqrt(D)
scale_hidden = 1.0 / math.sqrt(FF)

MESH = pl.DeviceIdType.MESH
F32 = jnp.float32
BF16 = jnp.bfloat16


def gelu_parts(value):
    inner = gelu_c * (value + gelu_k * value * value * value)
    tangent = jnp.tanh(inner)
    act = 0.5 * value * (1.0 + tangent)
    slope = 0.5 * (1.0 + tangent) + 0.5 * value * (1.0 - tangent * tangent) * gelu_c * (
        1.0 + 3.0 * gelu_k * value * value
    )
    return act, slope


def dot(left, right, dims):
    return lax.dot_general(left, right, (dims, ((), ())), preferred_element_type=F32)


def place_behind(k):
    return jnp.maximum(2 * k - 1, 0)


def place_ahead(k):
    return jnp.minimum(2 * k, 7)


def block_rows(place, pair):
    return pl.ds(pl.multiple_of(place * PAIR + BLOCK * pair, 16), BLOCK)


def pair_rows(place):
    return pl.ds(pl.multiple_of(place * PAIR, 16), PAIR)


def loop(first, end, step):
    def one(i, carry):
        step(i)
        return carry

    lax.fori_loop(first, end, one, 0)


def kernel(
    distance,
    x_in, cot_in, wg_in, wu_in, wd_in,
    grad_out, gate_out, up_out, down_out,
    xs, cs, weights, gu, hid, turned, gate_up, part, part_sib, lead, chain, new_buf, peer_buf, relay,
    wide32, pair32, ysend, ybuf, fin, rows32,
    load_sem, pair_ss, pair_rs, zx_ss, zx_rs, zc_ss, zc_rs, yx_ss, yx_rs, yc_ss, yc_rs,
    sx_ss, sx_rs, sc_ss, sc_rs, p_ss, p_rs, ch_ss, ch_rs, ys_ss, ys_rs, f_ss, f_rs,
    g_ss, g_rs, out_sem, r_ss, r_rs,
):
    r = lax.axis_index("replica")
    t = lax.axis_index("tensor")
    z, yh, c = t // 4, (t // 2) % 2, t % 2
    base = yh * 2 + c
    ahead = (r, lax.rem(z + 1, 8) * 4 + base)
    behind = (r, lax.rem(z + 7, 8) * 4 + base)
    across = (r, z * 4 + (1 - yh) * 2 + c)
    sibling = (r, z * 4 + yh * 2 + (1 - c))
    gives_to = (lax.rem(r + 8 - distance, 8), t)
    takes_from = (lax.rem(r + distance, 8), t)

    long = LONG if distance == 2 else 0
    onward = (r, lax.rem(z + 1 + 6 * c, 8) * 4 + base)
    backward_on = (r, lax.rem(z + 7 - 6 * c, 8) * 4 + base)

    mine = pl.ds(pl.multiple_of(c * HALF, 128), HALF)
    other = pl.ds(pl.multiple_of((1 - c) * HALF, 128), HALF)

    def remote(src, dst, ss, rs, device):
        return pltpu.make_async_remote_copy(
            src_ref=src, dst_ref=dst, send_sem=ss, recv_sem=rs, device_id=device, device_id_type=MESH
        )

    loads = [
        pltpu.make_async_copy(source.at[0], weights.at[pl.ds(WIDE * i, UNITS), :], load_sem.at[i])
        for i, source in enumerate((wg_in, wu_in, wd_in))
    ]
    for load in loads:
        load.start()

    barrier = pltpu.get_barrier_semaphore()
    senders = (ahead, behind, across, sibling, takes_from) + ((gives_to,) if long else ())
    for device in senders:
        pl.semaphore_signal(barrier, inc=1, device_id=device, device_id_type=MESH)
    wide32[0] = x_in[0].astype(F32)
    wide32[1] = cot_in[0].astype(F32)
    pl.semaphore_wait(barrier, len(senders))

    forty = pl.ds(pl.multiple_of(c * 40, 8), 40)
    pairs = [
        remote(wide32.at[a, :, other], pair32.at[a, forty, :], pair_ss.at[a], pair_rs.at[a], sibling) for a in range(2)
    ]
    for copy in pairs:
        copy.start()
    for a in range(2):
        pair32[a, forty, :] = wide32[a, :, mine]

    def first_place(k):
        return jnp.where(c == 0, place_behind(k), place_ahead(k))

    def second_place(k):
        return jnp.where(c == 0, place_ahead(k), place_behind(k))

    def hop(buf, ss, rs, forward, k, pair):
        place = first_place if forward else second_place
        slot = 2 * place(k) + pair
        return remote(
            buf.at[block_rows(place(k - 1), pair), mine], buf.at[block_rows(place(k), pair), mine],
            ss.at[slot], rs.at[slot], onward if forward else backward_on,
        )

    def x_hop(forward, k):
        return hop(xs, zx_ss, zx_rs, forward, k, 0)

    def c_hop(forward, k, pair):
        return hop(cs, zc_ss, zc_rs, forward, k, pair)

    def x_across(place):
        return remote(
            xs.at[block_rows(place, 0), mine], xs.at[block_rows(place, 1), mine],
            yx_ss.at[place], yx_rs.at[place], across,
        )

    c_across = remote(cs.at[block_rows(0, 0), mine], cs.at[block_rows(0, 1), mine], yc_ss, yc_rs, across)

    def x_sibling(place):
        at = xs.at[pair_rows(place), mine]
        return remote(at, at, sx_ss.at[place], sx_rs.at[place], sibling)

    def c_sibling(place):
        at = cs.at[pair_rows(place), mine]
        return remote(at, at, sc_ss.at[place], sc_rs.at[place], sibling)

    def part_sibling(place):
        rows = pair_rows(place)
        return remote(part.at[rows, other], part_sib.at[rows, :], p_ss.at[place], p_rs.at[place], sibling)

    pairs[0].wait_recv()
    xs[pl.ds(0, BLOCK), mine] = pair32[0].astype(BF16)
    x_hop(True, 1).start()
    x_hop(False, 1).start()
    x_across(0).start()
    pairs[1].wait_recv()
    cs[pl.ds(0, BLOCK), mine] = pair32[1].astype(BF16)
    c_across.start()

    for i in range(3):
        weights[pl.ds(WIDE * i + UNITS, WIDE - UNITS), :] = jnp.zeros((WIDE - UNITS, D), BF16)
    for load in loads:
        load.wait()

    def forward_a(place):
        x_sibling(place).wait_recv()
        gate_up[lax.rem(place, 4)] = dot(xs[pair_rows(place), :], weights[pl.ds(0, 2 * WIDE), :], ((1,), (1,)))

    def forward_b(place):
        c_sibling(place).wait_recv()
        at = lax.rem(place, 4)
        rows = pair_rows(place)
        hidden_grad = dot(cs[rows, :], weights[pl.ds(2 * WIDE, WIDE), :], ((1,), (1,))) * scale_hidden
        gate = gate_up[at, :, pl.ds(0, WIDE)] * scale_model
        up = gate_up[at, :, pl.ds(WIDE, WIDE)] * scale_model
        act, slope = gelu_parts(gate)
        hid[rows, :] = (act * up).astype(BF16)
        gu[rows, pl.ds(0, WIDE)] = (hidden_grad * up * slope).astype(BF16)
        gu[rows, pl.ds(WIDE, WIDE)] = (hidden_grad * act).astype(BF16)

    def turn(b):
        rows = pl.ds(pl.multiple_of(b * 128, 128), 128)
        turned[pl.ds(0, UNITS), rows] = gu[rows, pl.ds(0, WIDE)].T[0:UNITS]
        turned[pl.ds(UNITS, UNITS), rows] = gu[rows, pl.ds(WIDE, WIDE)].T[0:UNITS]
        turned[pl.ds(2 * UNITS, UNITS), rows] = hid[rows, :].T[0:UNITS]

    def turn_pair(place):
        loop((PAIR * place) // 128, (PAIR * (place + 1)) // 128, turn)

    def backward(place):
        rows = pair_rows(place)

        def columns(j):
            cols = pl.ds(pl.multiple_of(j * 768, 768), 768)
            part[rows, cols] = dot(gu[rows, :], weights[pl.ds(0, 2 * WIDE), cols], ((1,), (0,)))

        loop(0, 3, columns)
        part_sibling(place).start()

    def gossip(j):
        return remote(new_buf.at[j], peer_buf.at[j], g_ss.at[j], g_rs.at[j], gives_to)

    def goes_long(j):
        return jnp.logical_and(j >= 1, j <= long)

    def long_way(hop_number, j):
        src = new_buf.at[j] if hop_number == 0 else relay.at[hop_number - 1, j - 1]
        if hop_number == 2:
            return remote(src, peer_buf.at[j], r_ss.at[2, j - 1], g_rs.at[j], takes_from)
        return remote(
            src, relay.at[hop_number, j - 1], r_ss.at[hop_number, j - 1], r_rs.at[hop_number, j - 1], takes_from
        )

    def pass_on(hop_number):
        def one(j):
            long_way(hop_number - 1, j).wait_recv()
            long_way(hop_number, j).start()

        loop(1, long + 1, one)

    def update(j):
        cols = pl.ds(pl.multiple_of(j * PIECE, PIECE), PIECE)
        sums = dot(turned[pl.ds(0, 2 * UNITS), :], xs[:, cols], ((1,), (0,))) * scale_model
        for i in range(2):
            old = weights[pl.ds(WIDE * i, UNITS), cols].astype(F32)
            new_buf[j, pl.ds(UNITS * i, UNITS), :] = (old - learn_rate * sums[UNITS * i : UNITS * (i + 1)]).astype(BF16)
        sums = dot(turned[pl.ds(2 * UNITS, UNITS), :], cs[:, cols], ((1,), (0,))) * scale_hidden
        old = weights[pl.ds(2 * WIDE, UNITS), cols].astype(F32)
        new_buf[j, pl.ds(2 * UNITS, UNITS), :] = (old - learn_rate * sums).astype(BF16)
        if long:
            @pl.when(goes_long(j))
            def _():
                long_way(0, j).start()

            pl.when(jnp.logical_not(goes_long(j)))(lambda: gossip(j).start())
        else:
            gossip(j).start()

    chains = ((True, 0, 4), (True, 1, 3), (False, 0, 3), (False, 1, 4))

    def stop_place(n, m):
        onward = chains[n][2] - m
        return place_ahead(onward) if chains[n][0] else place_behind(onward)

    def chain_hop(n, m, src):
        return remote(src, chain.at[n, m], ch_ss.at[n, m], ch_rs.at[n, m], ahead if chains[n][0] else behind)

    def add_share(dst, src, place, pair):
        def some(i):
            at = pl.ds(pl.multiple_of(i * 16, 16), 16)
            rows = pl.ds(pl.multiple_of(place * PAIR + BLOCK * pair + i * 16, 16), 16)
            share = part[rows, mine] + part_sib[rows, :]
            dst[at, :] = (share if src is None else src(at) + share).astype(dst.dtype)

        loop(0, BLOCK // 16, some)

    def start_chains():
        for p in (5, 6, 7):
            part_sibling(p).wait_recv()
        for n, (_, pair, _) in enumerate(chains):
            place = stop_place(n, 0)
            add_share(lead.at[n], None, place, pair)
            chain_hop(n, 0, lead.at[n]).start()

    def places(k, work):
        loop(jnp.maximum(2 * k - 1, 0), jnp.where(k < 0, 0, jnp.minimum(2 * k + 1, 8)), work)

    def step(k):
        @pl.when(k <= 4)
        def _():
            x_hop(True, k).wait_recv()

            @pl.when(k <= 3)
            def _():
                x_hop(True, k + 1).start()

            x_across(first_place(k)).start()

            @pl.when(k <= 3)
            def _():
                x_hop(False, k).wait_recv()

                @pl.when(k <= 2)
                def _():
                    x_hop(False, k + 1).start()

                x_across(second_place(k)).start()

        def from_across(place):
            x_across(place).wait_recv()
            x_sibling(place).start()

        def take_c(forward, pair):
            far = forward == (pair == 0)

            @pl.when(k <= (5 if far else 4))
            def _():
                @pl.when(k >= 2)
                def _():
                    c_hop(forward, k - 1, pair).wait_recv()

                @pl.when(k <= (4 if far else 3))
                def _():
                    c_hop(forward, k, pair).start()

        places(k - 1, from_across)
        take_c(True, 0)
        take_c(False, 0)
        places(k - 1, forward_a)
        places(k - 2, forward_b)

        @pl.when(k == 1)
        def _():
            c_across.wait_recv()

        take_c(False, 1)
        take_c(True, 1)
        places(k - 1, lambda place: c_sibling(place).start())
        places(k - 2, turn_pair)

        @pl.when(k == 7)
        def _():
            backward(7)
            start_chains()

        loop(jnp.where(k == 7, EARLY, 0), jnp.where(k == 7, PIECES, jnp.where(k == 6, EARLY, 0)), update)

        @pl.when(k < 7)
        def _():
            places(k - 3, backward)

    loop(1, 8, step)

    for p in range(5):
        part_sibling(p).wait_recv()

    def chain_step(m):
        for n, (_, pair, stops) in enumerate(chains):
            def go(n=n, pair=pair):
                at = chain.at[n, m - 1]
                chain_hop(n, m - 1, at).wait_recv()
                add_share(at, lambda i: at[i, :].astype(F32), stop_place(n, m), pair)
                chain_hop(n, m, at).start()

            if stops == 4:
                go()
            elif isinstance(m, int):
                if m < stops:
                    go()
            else:
                pl.when(m < stops)(go)

    if long:
        loop(1, 3, chain_step)
        pass_on(1)
        chain_step(3)
    else:
        loop(1, 4, chain_step)
    for n in (1, 3):
        chain_hop(n, chains[n][2] - 1, chain.at[n, 0]).wait_recv()
    add_share(ysend, lambda i: chain[1, 2, i, :].astype(F32) + chain[3, 3, i, :].astype(F32), 0, 1)
    y_sum = remote(ysend, ybuf, ys_ss, ys_rs, across)
    y_sum.start()
    for n in (0, 2):
        chain_hop(n, chains[n][2] - 1, chain.at[n, 0]).wait_recv()
    add_share(fin, lambda i: chain[0, 3, i, :].astype(F32) + chain[2, 2, i, :].astype(F32), 0, 0)
    y_sum.wait_recv()
    fin[...] = (fin[...] + ybuf[...]) * scale_model
    theirs = pl.ds(pl.multiple_of((1 - c) * 40, 8), 40)
    rows_fly = remote(fin.at[theirs, :], rows32.at[:, mine], f_ss, f_rs, sibling)
    rows_fly.start()
    rows32[:, mine] = fin[forty, :]
    rows_fly.wait_recv()
    grad_out[0] = rows32[...].astype(BF16)

    def outs(j):
        cols = pl.ds(pl.multiple_of(j * PIECE, PIECE), PIECE)
        return [
            pltpu.make_async_copy(peer_buf.at[j, pl.ds(UNITS * i, UNITS), :], out.at[0, :, cols], out_sem.at[i, j])
            for i, out in enumerate((gate_out, up_out, down_out))
        ]

    def mean_step(i):
        j = lax.rem(i + long + 1, PIECES) if long else i
        gossip(j).wait_recv()

        def some(i):
            at = pl.ds(pl.multiple_of(i * 144, 16), 144)
            mean = (new_buf[j, at, :].astype(F32) + peer_buf[j, at, :].astype(F32)) * 0.5
            peer_buf[j, at, :] = mean.astype(BF16)

        loop(0, 3 * UNITS // 144, some)
        for copy in outs(j):
            copy.start()

    if long:
        pass_on(2)
    loop(0, PIECES, mean_step)

    for copy in (*pairs, c_across, y_sum, rows_fly):
        copy.wait_send()

    def sent(place):
        x_across(place).wait_send()
        x_sibling(place).wait_send()
        c_sibling(place).wait_send()
        part_sibling(place).wait_send()

    loop(0, 8, sent)

    def hops_sent(k):
        x_hop(True, k).wait_send()
        c_hop(True, k, 0).wait_send()
        c_hop(False, k, 1).wait_send()
        chain_hop(0, k - 1, chain.at[0, 0]).wait_send()
        chain_hop(3, k - 1, chain.at[0, 0]).wait_send()

        @pl.when(k <= 3)
        def _():
            x_hop(False, k).wait_send()
            c_hop(True, k, 1).wait_send()
            c_hop(False, k, 0).wait_send()
            chain_hop(1, k - 1, chain.at[0, 0]).wait_send()
            chain_hop(2, k - 1, chain.at[0, 0]).wait_send()

    loop(1, 5, hops_sent)

    def finish(j):
        if long:
            @pl.when(goes_long(j))
            def _():
                for hop_number in range(3):
                    long_way(hop_number, j).wait_send()

            pl.when(jnp.logical_not(goes_long(j)))(lambda: gossip(j).wait_send())
        else:
            gossip(j).wait_send()
        for copy in outs(j):
            copy.wait()

    loop(0, PIECES, finish)


def call(distance, arrays):
    dma = pltpu.SemaphoreType.DMA
    link = BF16 if distance == 2 else F32
    vmem = pl.BlockSpec(memory_space=pltpu.VMEM)
    hbm = pl.BlockSpec(memory_space=pl.ANY)
    return pl.pallas_call(
        functools.partial(kernel, distance),
        out_shape=(jax.ShapeDtypeStruct((1, 40, D), BF16),) + (jax.ShapeDtypeStruct((1, UNITS, D), BF16),) * 3,
        in_specs=[vmem, vmem, hbm, hbm, hbm],
        out_specs=(vmem, hbm, hbm, hbm),
        scratch_shapes=[
            pltpu.VMEM((TOKENS, D), BF16),
            pltpu.VMEM((TOKENS, D), BF16),
            pltpu.VMEM((3 * WIDE, D), BF16),
            pltpu.VMEM((TOKENS, 2 * WIDE), BF16),
            pltpu.VMEM((TOKENS, WIDE), BF16),
            pltpu.VMEM((3 * UNITS, TOKENS), BF16),
            pltpu.VMEM((4, PAIR, 2 * WIDE), F32),
            pltpu.VMEM((TOKENS, D), F32),
            pltpu.VMEM((TOKENS, HALF), F32),
            pltpu.VMEM((4, BLOCK, HALF), link),
            pltpu.VMEM((4, 4, BLOCK, HALF), link),
            pltpu.VMEM((PIECES, 3 * UNITS, PIECE), BF16),
            pltpu.VMEM((PIECES, 3 * UNITS, PIECE), BF16),
            pltpu.VMEM((2, LONG, 3 * UNITS, PIECE) if distance == 2 else (2, LONG, 16, 128), BF16),
            pltpu.VMEM((2, 40, D), F32),
            pltpu.VMEM((2, BLOCK, HALF), F32),
            pltpu.VMEM((BLOCK, HALF), F32),
            pltpu.VMEM((BLOCK, HALF), F32),
            pltpu.VMEM((BLOCK, HALF), F32),
            pltpu.VMEM((40, D), F32),
            dma((3,)), dma((2,)), dma((2,)),
            dma((16,)), dma((16,)), dma((16,)), dma((16,)), dma((8,)), dma((8,)), dma, dma,
            dma((8,)), dma((8,)), dma((8,)), dma((8,)), dma((8,)), dma((8,)), dma((4, 4)), dma((4, 4)),
            dma, dma, dma, dma,
            dma((PIECES,)), dma((PIECES,)), dma((3, PIECES)), dma((3, LONG)), dma((2, LONG)),
        ],
        compiler_params=pltpu.CompilerParams(
            collective_id=distance, has_side_effects=True, vmem_limit_bytes=63 * 2**20
        ),
        cost_estimate=pl.CostEstimate(flops=13600000000, bytes_accessed=10000000, transcendentals=400000),
        name=f"gossip_by_{distance}",
    )(*arrays)


def hand_over_kernel(*refs):
    sources, results, (held, in_sem, out_sem) = refs[:3], refs[3:6], refs[6:]
    spots = [(i, j, pl.ds(96 * j, 96)) for i in range(3) for j in range(3)]
    ins = [pltpu.make_async_copy(sources[i].at[0, at, :], held.at[i, at, :], in_sem.at[i, j]) for i, j, at in spots]
    outs = [pltpu.make_async_copy(held.at[i, at, :], results[i].at[0, at, :], out_sem.at[i, j]) for i, j, at in spots]
    for copy in ins:
        copy.start()
    for arrived, leaving in zip(ins, outs):
        arrived.wait()
        leaving.start()
    for copy in outs:
        copy.wait()


def hand_over(arrays):
    hbm = pl.BlockSpec(memory_space=pl.ANY)
    return pl.pallas_call(
        hand_over_kernel,
        out_shape=(jax.ShapeDtypeStruct((1, UNITS, D), BF16),) * 3,
        in_specs=[hbm] * 3,
        out_specs=(hbm,) * 3,
        scratch_shapes=[
            pltpu.VMEM((3, UNITS, D), BF16),
            pltpu.SemaphoreType.DMA((3, 3)),
            pltpu.SemaphoreType.DMA((3, 3)),
        ],
        compiler_params=pltpu.CompilerParams(vmem_limit_bytes=63 * 2**20),
        name="hand_over",
    )(*arrays)


def body(inputs, cotangent, gate_weight, up_weight, down_weight, step):
    arrays = (
        inputs, cotangent, jnp.swapaxes(gate_weight, 1, 2), jnp.swapaxes(up_weight, 1, 2), down_weight,
    )
    branches = [functools.partial(call, 1 << power) for power in range(3)]
    grad, *means = lax.switch(step[0] % 3, branches, arrays)
    gate, up, down = hand_over(means)
    return grad, jnp.swapaxes(gate, 1, 2), jnp.swapaxes(up, 1, 2), down


def solution(mesh):
    in_specs = (
        P("replica", "tensor", None),
        P("replica", "tensor", None),
        P("replica", None, "tensor"),
        P("replica", None, "tensor"),
        P("replica", "tensor", None),
        P(),
    )
    out_specs = (
        P("replica", "tensor", None),
        P("replica", None, "tensor"),
        P("replica", None, "tensor"),
        P("replica", "tensor", None),
    )
    return jax.shard_map(body, mesh=mesh, in_specs=in_specs, out_specs=out_specs, check_vma=False)
```

```python
import functools
import math

import jax
import jax.numpy as jnp
from jax import lax
from jax.experimental import pallas as pl
from jax.experimental.pallas import tpu as pltpu
from jax.sharding import PartitionSpec as P

D = 2304
FF = 9216
TOKENS = 1280
UNITS = 288
WIDE = 384
BLOCK = 80
PAIR = 160
HALF = D // 2
PIECE = 256
PIECES = D // PIECE
EARLY = 4
LONG = 2

gelu_c = 0.7978845608028654
gelu_k = 0.044715
learn_rate = 1.0
scale_model = 1.0 / math.sqrt(D)
scale_hidden = 1.0 / math.sqrt(FF)

MESH = pl.DeviceIdType.MESH
F32 = jnp.float32
BF16 = jnp.bfloat16


def gelu_parts(value):
    inner = gelu_c * (value + gelu_k * value * value * value)
    tangent = jnp.tanh(inner)
    act = 0.5 * value * (1.0 + tangent)
    slope = 0.5 * (1.0 + tangent) + 0.5 * value * (1.0 - tangent * tangent) * gelu_c * (
        1.0 + 3.0 * gelu_k * value * value
    )
    return act, slope


def dot(left, right, dims):
    return lax.dot_general(left, right, (dims, ((), ())), preferred_element_type=F32)


def place_behind(k):
    return jnp.maximum(2 * k - 1, 0)


def place_ahead(k):
    return jnp.minimum(2 * k, 7)


def block_rows(place, pair):
    return pl.ds(pl.multiple_of(place * PAIR + BLOCK * pair, 16), BLOCK)


def pair_rows(place):
    return pl.ds(pl.multiple_of(place * PAIR, 16), PAIR)


def loop(first, end, step):
    def one(i, carry):
        step(i)
        return carry

    lax.fori_loop(first, end, one, 0)


def kernel(
    distance,
    x_in, cot_in, wg_in, wu_in, wd_in,
    grad_out, gate_out, up_out, down_out,
    xs, cs, weights, gu, hid, turned, gate_up, part, part_sib, lead, chain, new_buf, peer_buf, relay,
    wide32, pair32, ysend, ybuf, fin, rows32,
    load_sem, pair_ss, pair_rs, zx_ss, zx_rs, zc_ss, zc_rs, yx_ss, yx_rs, yc_ss, yc_rs,
    sx_ss, sx_rs, sc_ss, sc_rs, p_ss, p_rs, ch_ss, ch_rs, ys_ss, ys_rs, f_ss, f_rs,
    g_ss, g_rs, out_sem, r_ss, r_rs,
):
    r = lax.axis_index("replica")
    t = lax.axis_index("tensor")
    z, yh, c = t // 4, (t // 2) % 2, t % 2
    base = yh * 2 + c
    ahead = (r, lax.rem(z + 1, 8) * 4 + base)
    behind = (r, lax.rem(z + 7, 8) * 4 + base)
    across = (r, z * 4 + (1 - yh) * 2 + c)
    sibling = (r, z * 4 + yh * 2 + (1 - c))
    gives_to = (lax.rem(r + 8 - distance, 8), t)
    takes_from = (lax.rem(r + distance, 8), t)

    long = LONG if distance == 2 else 0
    early = EARLY + (1 if long else 0)
    onward = (r, lax.rem(z + 1 + 6 * c, 8) * 4 + base)
    backward_on = (r, lax.rem(z + 7 - 6 * c, 8) * 4 + base)

    mine = pl.ds(pl.multiple_of(c * HALF, 128), HALF)
    other = pl.ds(pl.multiple_of((1 - c) * HALF, 128), HALF)

    def remote(src, dst, ss, rs, device):
        return pltpu.make_async_remote_copy(
            src_ref=src, dst_ref=dst, send_sem=ss, recv_sem=rs, device_id=device, device_id_type=MESH
        )

    loads = [
        pltpu.make_async_copy(source.at[0], weights.at[pl.ds(WIDE * i, UNITS), :], load_sem.at[i])
        for i, source in enumerate((wg_in, wu_in, wd_in))
    ]
    for load in loads:
        load.start()

    barrier = pltpu.get_barrier_semaphore()
    senders = (ahead, behind, across, sibling, takes_from) + ((gives_to,) if long else ())
    for device in senders:
        pl.semaphore_signal(barrier, inc=1, device_id=device, device_id_type=MESH)
    wide32[0] = x_in[0].astype(F32)
    wide32[1] = cot_in[0].astype(F32)
    pl.semaphore_wait(barrier, len(senders))

    forty = pl.ds(pl.multiple_of(c * 40, 8), 40)
    pairs = [
        remote(wide32.at[a, :, other], pair32.at[a, forty, :], pair_ss.at[a], pair_rs.at[a], sibling) for a in range(2)
    ]
    for copy in pairs:
        copy.start()
    for a in range(2):
        pair32[a, forty, :] = wide32[a, :, mine]

    def first_place(k):
        return jnp.where(c == 0, place_behind(k), place_ahead(k))

    def second_place(k):
        return jnp.where(c == 0, place_ahead(k), place_behind(k))

    def hop(buf, ss, rs, forward, k, pair):
        place = first_place if forward else second_place
        slot = 2 * place(k) + pair
        return remote(
            buf.at[block_rows(place(k - 1), pair), mine], buf.at[block_rows(place(k), pair), mine],
            ss.at[slot], rs.at[slot], onward if forward else backward_on,
        )

    def x_hop(forward, k):
        return hop(xs, zx_ss, zx_rs, forward, k, 0)

    def c_hop(forward, k, pair):
        return hop(cs, zc_ss, zc_rs, forward, k, pair)

    def x_across(place):
        return remote(
            xs.at[block_rows(place, 0), mine], xs.at[block_rows(place, 1), mine],
            yx_ss.at[place], yx_rs.at[place], across,
        )

    c_across = remote(cs.at[block_rows(0, 0), mine], cs.at[block_rows(0, 1), mine], yc_ss, yc_rs, across)

    def x_sibling(place):
        at = xs.at[pair_rows(place), mine]
        return remote(at, at, sx_ss.at[place], sx_rs.at[place], sibling)

    def c_sibling(place):
        at = cs.at[pair_rows(place), mine]
        return remote(at, at, sc_ss.at[place], sc_rs.at[place], sibling)

    def part_sibling(place):
        rows = pair_rows(place)
        return remote(part.at[rows, other], part_sib.at[rows, :], p_ss.at[place], p_rs.at[place], sibling)

    pairs[0].wait_recv()
    xs[pl.ds(0, BLOCK), mine] = pair32[0].astype(BF16)
    x_hop(True, 1).start()
    x_hop(False, 1).start()
    x_across(0).start()
    pairs[1].wait_recv()
    cs[pl.ds(0, BLOCK), mine] = pair32[1].astype(BF16)
    c_across.start()

    for i in range(3):
        weights[pl.ds(WIDE * i + UNITS, WIDE - UNITS), :] = jnp.zeros((WIDE - UNITS, D), BF16)
    for forward in (True, False):
        c_hop(forward, 1, 0).start()
    for load in loads:
        load.wait()

    def forward_a(place):
        x_sibling(place).wait_recv()
        gate_up[lax.rem(place, 4)] = dot(xs[pair_rows(place), :], weights[pl.ds(0, 2 * WIDE), :], ((1,), (1,)))

    def forward_b(place):
        c_sibling(place).wait_recv()
        at = lax.rem(place, 4)
        rows = pair_rows(place)
        hidden_grad = dot(cs[rows, :], weights[pl.ds(2 * WIDE, WIDE), :], ((1,), (1,))) * scale_hidden
        gate = gate_up[at, :, pl.ds(0, WIDE)] * scale_model
        up = gate_up[at, :, pl.ds(WIDE, WIDE)] * scale_model
        act, slope = gelu_parts(gate)
        hid[rows, :] = (act * up).astype(BF16)
        gu[rows, pl.ds(0, WIDE)] = (hidden_grad * up * slope).astype(BF16)
        gu[rows, pl.ds(WIDE, WIDE)] = (hidden_grad * act).astype(BF16)

    def turn(b):
        rows = pl.ds(pl.multiple_of(b * 128, 128), 128)
        turned[pl.ds(0, UNITS), rows] = gu[rows, pl.ds(0, WIDE)].T[0:UNITS]
        turned[pl.ds(UNITS, UNITS), rows] = gu[rows, pl.ds(WIDE, WIDE)].T[0:UNITS]
        turned[pl.ds(2 * UNITS, UNITS), rows] = hid[rows, :].T[0:UNITS]

    def turn_pair(place):
        loop((PAIR * place) // 128, (PAIR * (place + 1)) // 128, turn)

    def backward(place):
        rows = pair_rows(place)

        def columns(j):
            cols = pl.ds(pl.multiple_of(j * 768, 768), 768)
            part[rows, cols] = dot(gu[rows, :], weights[pl.ds(0, 2 * WIDE), cols], ((1,), (0,)))

        loop(0, 3, columns)
        part_sibling(place).start()

    def gossip(j):
        return remote(new_buf.at[j], peer_buf.at[j], g_ss.at[j], g_rs.at[j], gives_to)

    def goes_long(j):
        return jnp.logical_and(j >= 1, j <= long)

    def long_way(hop_number, j):
        src = new_buf.at[j] if hop_number == 0 else relay.at[hop_number - 1, j - 1]
        if hop_number == 2:
            return remote(src, peer_buf.at[j], r_ss.at[2, j - 1], g_rs.at[j], takes_from)
        return remote(
            src, relay.at[hop_number, j - 1], r_ss.at[hop_number, j - 1], r_rs.at[hop_number, j - 1], takes_from
        )

    def pass_on(hop_number):
        def one(j):
            long_way(hop_number - 1, j).wait_recv()
            long_way(hop_number, j).start()

        loop(1, long + 1, one)

    def update(j):
        cols = pl.ds(pl.multiple_of(j * PIECE, PIECE), PIECE)
        sums = dot(turned[pl.ds(0, 2 * UNITS), :], xs[:, cols], ((1,), (0,))) * scale_model
        for i in range(2):
            old = weights[pl.ds(WIDE * i, UNITS), cols].astype(F32)
            new_buf[j, pl.ds(UNITS * i, UNITS), :] = (old - learn_rate * sums[UNITS * i : UNITS * (i + 1)]).astype(BF16)
        sums = dot(turned[pl.ds(2 * UNITS, UNITS), :], cs[:, cols], ((1,), (0,))) * scale_hidden
        old = weights[pl.ds(2 * WIDE, UNITS), cols].astype(F32)
        new_buf[j, pl.ds(2 * UNITS, UNITS), :] = (old - learn_rate * sums).astype(BF16)
        if long:
            @pl.when(goes_long(j))
            def _():
                long_way(0, j).start()

            pl.when(jnp.logical_not(goes_long(j)))(lambda: gossip(j).start())
        else:
            gossip(j).start()

    chains = ((True, 0, 4), (True, 1, 3), (False, 0, 3), (False, 1, 4))

    def stop_place(n, m):
        onward = chains[n][2] - m
        return place_ahead(onward) if chains[n][0] else place_behind(onward)

    def chain_hop(n, m, src):
        return remote(src, chain.at[n, m], ch_ss.at[n, m], ch_rs.at[n, m], ahead if chains[n][0] else behind)

    def add_share(dst, src, place, pair):
        def some(i):
            at = pl.ds(pl.multiple_of(i * 16, 16), 16)
            rows = pl.ds(pl.multiple_of(place * PAIR + BLOCK * pair + i * 16, 16), 16)
            share = part[rows, mine] + part_sib[rows, :]
            dst[at, :] = (share if src is None else src(at) + share).astype(dst.dtype)

        loop(0, BLOCK // 16, some)

    def start_chains():
        for p in range(8):
            part_sibling(p).wait_recv()
        for n, (_, pair, _) in enumerate(chains):
            place = stop_place(n, 0)
            add_share(lead.at[n], None, place, pair)
            chain_hop(n, 0, lead.at[n]).start()

    def chain_step(m):
        for n, (_, pair, stops) in enumerate(chains):
            def go(n=n, pair=pair):
                at = chain.at[n, m - 1]
                chain_hop(n, m - 1, at).wait_recv()
                add_share(at, lambda i: at[i, :].astype(F32), stop_place(n, m), pair)
                chain_hop(n, m, at).start()

            if stops == 4:
                go()
            else:
                pl.when(m < stops)(go)

    def places(k, work):
        loop(jnp.maximum(2 * k - 1, 0), jnp.where(k < 0, 0, jnp.minimum(2 * k + 1, 8)), work)

    def step(k):
        @pl.when(k <= 4)
        def _():
            x_hop(True, k).wait_recv()

            @pl.when(k <= 3)
            def _():
                x_hop(True, k + 1).start()

            x_across(first_place(k)).start()

            @pl.when(k <= 3)
            def _():
                x_hop(False, k).wait_recv()

                @pl.when(k <= 2)
                def _():
                    x_hop(False, k + 1).start()

                x_across(second_place(k)).start()

        def from_across(place):
            x_across(place).wait_recv()
            x_sibling(place).start()

        def take_c(forward, pair):
            far = forward == (pair == 0)

            @pl.when(k <= (5 if far else 4))
            def _():
                @pl.when(k >= 2)
                def _():
                    c_hop(forward, k - 1, pair).wait_recv()

                @pl.when(jnp.logical_and(k <= (4 if far else 3), k >= (2 if pair == 0 else 1)))
                def _():
                    c_hop(forward, k, pair).start()

        places(k - 1, from_across)
        take_c(True, 0)
        take_c(False, 0)
        places(k - 1, forward_a)

        @pl.when(k == 1)
        def _():
            c_across.wait_recv()

        take_c(False, 1)
        take_c(True, 1)
        places(k - 1, lambda place: c_sibling(place).start())
        places(k - 2, forward_b)
        places(k - 2, turn_pair)

        @pl.when(k == 7)
        def _():
            backward(7)
            start_chains()

        @pl.when(k >= 8)
        def _():
            chain_step(k - 7)
            if long:
                pl.when(k == 8)(lambda: pass_on(1))

        done = jnp.where(k >= 8, early + 2 * (k - 8), 0)
        goal = jnp.where(k >= 8, jnp.minimum(done + 2, PIECES), jnp.where(k == 6, early, 0))
        loop(done, goal, update)

        @pl.when(k < 7)
        def _():
            places(k - 3, backward)

    loop(1, 11, step)

    for n in (1, 3):
        chain_hop(n, chains[n][2] - 1, chain.at[n, 0]).wait_recv()
    add_share(ysend, lambda i: chain[1, 2, i, :].astype(F32) + chain[3, 3, i, :].astype(F32), 0, 1)
    y_sum = remote(ysend, ybuf, ys_ss, ys_rs, across)
    y_sum.start()
    if long:
        pass_on(2)
    for n in (0, 2):
        chain_hop(n, chains[n][2] - 1, chain.at[n, 0]).wait_recv()
    add_share(fin, lambda i: chain[0, 3, i, :].astype(F32) + chain[2, 2, i, :].astype(F32), 0, 0)
    y_sum.wait_recv()
    fin[...] = (fin[...] + ybuf[...].astype(F32)) * scale_model
    theirs = pl.ds(pl.multiple_of((1 - c) * 40, 8), 40)
    rows_fly = remote(fin.at[theirs, :], rows32.at[:, mine], f_ss, f_rs, sibling)
    rows_fly.start()
    rows32[:, mine] = fin[forty, :]
    rows_fly.wait_recv()
    grad_out[0] = rows32[...].astype(BF16)

    for copy in (*pairs, c_across, y_sum, rows_fly):
        copy.wait_send()

    def sent(place):
        x_across(place).wait_send()
        x_sibling(place).wait_send()
        c_sibling(place).wait_send()
        part_sibling(place).wait_send()

    loop(0, 8, sent)

    def hops_sent(k):
        x_hop(True, k).wait_send()
        c_hop(True, k, 0).wait_send()
        c_hop(False, k, 1).wait_send()
        chain_hop(0, k - 1, chain.at[0, 0]).wait_send()
        chain_hop(3, k - 1, chain.at[0, 0]).wait_send()

        @pl.when(k <= 3)
        def _():
            x_hop(False, k).wait_send()
            c_hop(True, k, 1).wait_send()
            c_hop(False, k, 0).wait_send()
            chain_hop(1, k - 1, chain.at[0, 0]).wait_send()
            chain_hop(2, k - 1, chain.at[0, 0]).wait_send()

    loop(1, 5, hops_sent)

    def outs(j):
        cols = pl.ds(pl.multiple_of(j * PIECE, PIECE), PIECE)
        return [
            pltpu.make_async_copy(peer_buf.at[j, pl.ds(UNITS * i, UNITS), :], out.at[0, :, cols], out_sem.at[i])
            for i, out in enumerate((gate_out, up_out, down_out))
        ]

    def mean_step(i):
        j = lax.rem(i + long + 1, PIECES) if long else i
        gossip(j).wait_recv()

        def some(i):
            at = pl.ds(pl.multiple_of(i * 144, 16), 144)
            mean = (new_buf[j, at, :].astype(F32) + peer_buf[j, at, :].astype(F32)) * 0.5
            peer_buf[j, at, :] = mean.astype(BF16)

        loop(0, 3 * UNITS // 144, some)
        for copy in outs(j):
            copy.start()

    loop(0, PIECES, mean_step)

    def finish(j):
        if long:
            @pl.when(goes_long(j))
            def _():
                for hop_number in range(3):
                    long_way(hop_number, j).wait_send()

            pl.when(jnp.logical_not(goes_long(j)))(lambda: gossip(j).wait_send())
        else:
            gossip(j).wait_send()

    loop(0, PIECES, finish)
    for i, out in enumerate((gate_out, up_out, down_out)):
        pltpu.make_async_copy(out.at[0], out.at[0], out_sem.at[i]).wait()


def call(distance, arrays):
    dma = pltpu.SemaphoreType.DMA
    link = BF16 if distance == 2 else F32
    y_link = BF16 if distance == 1 else F32
    vmem = pl.BlockSpec(memory_space=pltpu.VMEM)
    hbm = pl.BlockSpec(memory_space=pl.ANY)
    return pl.pallas_call(
        functools.partial(kernel, distance),
        out_shape=(jax.ShapeDtypeStruct((1, 40, D), BF16),) + (jax.ShapeDtypeStruct((1, UNITS, D), BF16),) * 3,
        in_specs=[vmem, vmem, hbm, hbm, hbm],
        out_specs=(vmem, hbm, hbm, hbm),
        scratch_shapes=[
            pltpu.VMEM((TOKENS, D), BF16),
            pltpu.VMEM((TOKENS, D), BF16),
            pltpu.VMEM((3 * WIDE, D), BF16),
            pltpu.VMEM((TOKENS, 2 * WIDE), BF16),
            pltpu.VMEM((TOKENS, WIDE), BF16),
            pltpu.VMEM((3 * UNITS, TOKENS), BF16),
            pltpu.VMEM((4, PAIR, 2 * WIDE), F32),
            pltpu.VMEM((TOKENS, D), F32),
            pltpu.VMEM((TOKENS, HALF), F32),
            pltpu.VMEM((4, BLOCK, HALF), link),
            pltpu.VMEM((4, 4, BLOCK, HALF), link),
            pltpu.VMEM((PIECES, 3 * UNITS, PIECE), BF16),
            pltpu.VMEM((PIECES, 3 * UNITS, PIECE), BF16),
            pltpu.VMEM((2, LONG, 3 * UNITS, PIECE) if distance == 2 else (2, LONG, 16, 128), BF16),
            pltpu.VMEM((2, 40, D), F32),
            pltpu.VMEM((2, BLOCK, HALF), F32),
            pltpu.VMEM((BLOCK, HALF), y_link),
            pltpu.VMEM((BLOCK, HALF), y_link),
            pltpu.VMEM((BLOCK, HALF), F32),
            pltpu.VMEM((40, D), F32),
            dma((3,)), dma((2,)), dma((2,)),
            dma((16,)), dma((16,)), dma((16,)), dma((16,)), dma((8,)), dma((8,)), dma, dma,
            dma((8,)), dma((8,)), dma((8,)), dma((8,)), dma((8,)), dma((8,)), dma((4, 4)), dma((4, 4)),
            dma, dma, dma, dma,
            dma((PIECES,)), dma((PIECES,)), dma((3,)), dma((3, LONG)), dma((2, LONG)),
        ],
        compiler_params=pltpu.CompilerParams(
            collective_id=distance, has_side_effects=True, vmem_limit_bytes=63 * 2**20
        ),
        cost_estimate=pl.CostEstimate(flops=13600000000, bytes_accessed=10000000, transcendentals=400000),
        name=f"gossip_by_{distance}",
    )(*arrays)


def hand_over_kernel(*refs):
    sources, results, (held, in_sem, out_sem) = refs[:3], refs[3:6], refs[6:]
    spots = [(i, j, pl.ds(96 * j, 96)) for i in range(3) for j in range(3)]
    ins = [pltpu.make_async_copy(sources[i].at[0, at, :], held.at[i, at, :], in_sem.at[i, j]) for i, j, at in spots]
    outs = [pltpu.make_async_copy(held.at[i, at, :], results[i].at[0, at, :], out_sem.at[i, j]) for i, j, at in spots]
    for copy in ins:
        copy.start()
    for arrived, leaving in zip(ins, outs):
        arrived.wait()
        leaving.start()
    for copy in outs:
        copy.wait()


def hand_over(arrays):
    hbm = pl.BlockSpec(memory_space=pl.ANY)
    return pl.pallas_call(
        hand_over_kernel,
        out_shape=(jax.ShapeDtypeStruct((1, UNITS, D), BF16),) * 3,
        in_specs=[hbm] * 3,
        out_specs=(hbm,) * 3,
        scratch_shapes=[
            pltpu.VMEM((3, UNITS, D), BF16),
            pltpu.SemaphoreType.DMA((3, 3)),
            pltpu.SemaphoreType.DMA((3, 3)),
        ],
        compiler_params=pltpu.CompilerParams(vmem_limit_bytes=63 * 2**20),
        name="hand_over",
    )(*arrays)


def body(inputs, cotangent, gate_weight, up_weight, down_weight, step):
    arrays = (
        inputs, cotangent, jnp.swapaxes(gate_weight, 1, 2), jnp.swapaxes(up_weight, 1, 2), down_weight,
    )
    branches = [functools.partial(call, 1 << power) for power in range(3)]
    grad, *means = lax.switch(step[0] % 3, branches, arrays)
    gate, up, down = hand_over(means)
    return grad, jnp.swapaxes(gate, 1, 2), jnp.swapaxes(up, 1, 2), down


def solution(mesh):
    in_specs = (
        P("replica", "tensor", None),
        P("replica", "tensor", None),
        P("replica", None, "tensor"),
        P("replica", None, "tensor"),
        P("replica", "tensor", None),
        P(),
    )
    out_specs = (
        P("replica", "tensor", None),
        P("replica", None, "tensor"),
        P("replica", None, "tensor"),
        P("replica", "tensor", None),
    )
    return jax.shard_map(body, mesh=mesh, in_specs=in_specs, out_specs=out_specs, check_vma=False)
```

```python
import functools
import math

import jax
import jax.numpy as jnp
from jax import lax
from jax.experimental import pallas as pl
from jax.experimental.pallas import tpu as pltpu
from jax.sharding import PartitionSpec as P

D = 2304
FF = 9216
TOKENS = 1280
UNITS = 288
WIDE = 384
BLOCK = 80
PAIR = 160
HALF = D // 2
PIECE = 256
PIECES = D // PIECE
EARLY = 4
LONG = 2

gelu_c = 0.7978845608028654
gelu_k = 0.044715
learn_rate = 1.0
scale_model = 1.0 / math.sqrt(D)
scale_hidden = 1.0 / math.sqrt(FF)

MESH = pl.DeviceIdType.MESH
F32 = jnp.float32
BF16 = jnp.bfloat16


def gelu_parts(value):
    inner = gelu_c * (value + gelu_k * value * value * value)
    tangent = jnp.tanh(inner)
    act = 0.5 * value * (1.0 + tangent)
    slope = 0.5 * (1.0 + tangent) + 0.5 * value * (1.0 - tangent * tangent) * gelu_c * (
        1.0 + 3.0 * gelu_k * value * value
    )
    return act, slope


def dot(left, right, dims):
    return lax.dot_general(left, right, (dims, ((), ())), preferred_element_type=F32)


def place_behind(k):
    return jnp.maximum(2 * k - 1, 0)


def place_ahead(k):
    return jnp.minimum(2 * k, 7)


def block_rows(place, pair):
    return pl.ds(pl.multiple_of(place * PAIR + BLOCK * pair, 16), BLOCK)


def pair_rows(place):
    return pl.ds(pl.multiple_of(place * PAIR, 16), PAIR)


def loop(first, end, step):
    def one(i, carry):
        step(i)
        return carry

    lax.fori_loop(first, end, one, 0)


def kernel(
    distance,
    x_in, cot_in, wg_in, wu_in, wd_in,
    grad_out, gate_out, up_out, down_out,
    xs, cs, weights, gu, hid, turned, gate_up, part, part_sib, lead, chain, new_buf, peer_buf, relay,
    wide32, pair32, ysend, ybuf, fin, rows32,
    load_sem, pair_ss, pair_rs, zx_ss, zx_rs, zc_ss, zc_rs, yx_ss, yx_rs, yc_ss, yc_rs,
    sx_ss, sx_rs, sc_ss, sc_rs, p_ss, p_rs, ch_ss, ch_rs, ys_ss, ys_rs, f_ss, f_rs,
    g_ss, g_rs, out_sem, r_ss, r_rs,
):
    r = lax.axis_index("replica")
    t = lax.axis_index("tensor")
    z, yh, c = t // 4, (t // 2) % 2, t % 2
    base = yh * 2 + c
    ahead = (r, lax.rem(z + 1, 8) * 4 + base)
    behind = (r, lax.rem(z + 7, 8) * 4 + base)
    across = (r, z * 4 + (1 - yh) * 2 + c)
    sibling = (r, z * 4 + yh * 2 + (1 - c))
    gives_to = (lax.rem(r + 8 - distance, 8), t)
    takes_from = (lax.rem(r + distance, 8), t)

    long = LONG if distance == 2 else 0
    early = EARLY + (1 if long else 0)
    onward = (r, lax.rem(z + 1 + 6 * c, 8) * 4 + base)
    backward_on = (r, lax.rem(z + 7 - 6 * c, 8) * 4 + base)

    mine = pl.ds(pl.multiple_of(c * HALF, 128), HALF)
    other = pl.ds(pl.multiple_of((1 - c) * HALF, 128), HALF)

    def remote(src, dst, ss, rs, device):
        return pltpu.make_async_remote_copy(
            src_ref=src, dst_ref=dst, send_sem=ss, recv_sem=rs, device_id=device, device_id_type=MESH
        )

    loads = [
        pltpu.make_async_copy(source.at[0], weights.at[pl.ds(WIDE * i, UNITS), :], load_sem.at[i])
        for i, source in enumerate((wg_in, wu_in, wd_in))
    ]
    for load in loads:
        load.start()

    barrier = pltpu.get_barrier_semaphore()
    senders = (ahead, behind, across, sibling, takes_from) + ((gives_to,) if long else ())
    for device in senders:
        pl.semaphore_signal(barrier, inc=1, device_id=device, device_id_type=MESH)
    wide32[0] = x_in[0].astype(F32)
    wide32[1] = cot_in[0].astype(F32)
    pl.semaphore_wait(barrier, len(senders))

    forty = pl.ds(pl.multiple_of(c * 40, 8), 40)
    pairs = [
        remote(wide32.at[a, :, other], pair32.at[a, forty, :], pair_ss.at[a], pair_rs.at[a], sibling) for a in range(2)
    ]
    for copy in pairs:
        copy.start()
    for a in range(2):
        pair32[a, forty, :] = wide32[a, :, mine]

    def first_place(k):
        return jnp.where(c == 0, place_behind(k), place_ahead(k))

    def second_place(k):
        return jnp.where(c == 0, place_ahead(k), place_behind(k))

    def hop(buf, ss, rs, forward, k, pair):
        place = first_place if forward else second_place
        slot = 2 * place(k) + pair
        return remote(
            buf.at[block_rows(place(k - 1), pair), mine], buf.at[block_rows(place(k), pair), mine],
            ss.at[slot], rs.at[slot], onward if forward else backward_on,
        )

    def x_hop(forward, k):
        return hop(xs, zx_ss, zx_rs, forward, k, 0)

    def c_hop(forward, k, pair):
        return hop(cs, zc_ss, zc_rs, forward, k, pair)

    def x_across(place):
        return remote(
            xs.at[block_rows(place, 0), mine], xs.at[block_rows(place, 1), mine],
            yx_ss.at[place], yx_rs.at[place], across,
        )

    c_across = remote(cs.at[block_rows(0, 0), mine], cs.at[block_rows(0, 1), mine], yc_ss, yc_rs, across)

    def x_sibling(place):
        at = xs.at[pair_rows(place), mine]
        return remote(at, at, sx_ss.at[place], sx_rs.at[place], sibling)

    def c_sibling(place):
        at = cs.at[pair_rows(place), mine]
        return remote(at, at, sc_ss.at[place], sc_rs.at[place], sibling)

    def part_sibling(place):
        rows = pair_rows(place)
        return remote(part.at[rows, other], part_sib.at[rows, :], p_ss.at[place], p_rs.at[place], sibling)

    pairs[0].wait_recv()
    xs[pl.ds(0, BLOCK), mine] = pair32[0].astype(BF16)
    x_hop(True, 1).start()
    x_hop(False, 1).start()
    x_across(0).start()
    pairs[1].wait_recv()
    cs[pl.ds(0, BLOCK), mine] = pair32[1].astype(BF16)
    c_across.start()

    for i in range(3):
        weights[pl.ds(WIDE * i + UNITS, WIDE - UNITS), :] = jnp.zeros((WIDE - UNITS, D), BF16)
    for forward in (True, False):
        c_hop(forward, 1, 0).start()
    for load in loads:
        load.wait()

    def forward_a(place):
        x_sibling(place).wait_recv()
        gate_up[lax.rem(place, 4)] = dot(xs[pair_rows(place), :], weights[pl.ds(0, 2 * WIDE), :], ((1,), (1,)))

    def forward_b(place):
        c_sibling(place).wait_recv()
        at = lax.rem(place, 4)
        rows = pair_rows(place)
        hidden_grad = dot(cs[rows, :], weights[pl.ds(2 * WIDE, WIDE), :], ((1,), (1,))) * scale_hidden
        gate = gate_up[at, :, pl.ds(0, WIDE)] * scale_model
        up = gate_up[at, :, pl.ds(WIDE, WIDE)] * scale_model
        act, slope = gelu_parts(gate)
        hid[rows, :] = (act * up).astype(BF16)
        gu[rows, pl.ds(0, WIDE)] = (hidden_grad * up * slope).astype(BF16)
        gu[rows, pl.ds(WIDE, WIDE)] = (hidden_grad * act).astype(BF16)

    def turn(b):
        rows = pl.ds(pl.multiple_of(b * 128, 128), 128)
        turned[pl.ds(0, UNITS), rows] = gu[rows, pl.ds(0, WIDE)].T[0:UNITS]
        turned[pl.ds(UNITS, UNITS), rows] = gu[rows, pl.ds(WIDE, WIDE)].T[0:UNITS]
        turned[pl.ds(2 * UNITS, UNITS), rows] = hid[rows, :].T[0:UNITS]

    def turn_pair(place):
        loop((PAIR * place) // 128, (PAIR * (place + 1)) // 128, turn)

    def backward(place):
        rows = pair_rows(place)

        def columns(j):
            cols = pl.ds(pl.multiple_of(j * 768, 768), 768)
            part[rows, cols] = dot(gu[rows, :], weights[pl.ds(0, 2 * WIDE), cols], ((1,), (0,)))

        loop(0, 3, columns)
        part_sibling(place).start()

    def gossip(j):
        return remote(new_buf.at[j], peer_buf.at[j], g_ss.at[j], g_rs.at[j], gives_to)

    def goes_long(j):
        return jnp.logical_and(j >= 1, j <= long)

    def long_way(hop_number, j):
        src = new_buf.at[j] if hop_number == 0 else relay.at[hop_number - 1, j - 1]
        if hop_number == 2:
            return remote(src, peer_buf.at[j], r_ss.at[2, j - 1], g_rs.at[j], takes_from)
        return remote(
            src, relay.at[hop_number, j - 1], r_ss.at[hop_number, j - 1], r_rs.at[hop_number, j - 1], takes_from
        )

    def pass_on(hop_number):
        def one(j):
            long_way(hop_number - 1, j).wait_recv()
            long_way(hop_number, j).start()

        loop(1, long + 1, one)

    def update(j):
        cols = pl.ds(pl.multiple_of(j * PIECE, PIECE), PIECE)
        sums = dot(turned[pl.ds(0, 2 * UNITS), :], xs[:, cols], ((1,), (0,))) * scale_model
        for i in range(2):
            old = weights[pl.ds(WIDE * i, UNITS), cols].astype(F32)
            new_buf[j, pl.ds(UNITS * i, UNITS), :] = (old - learn_rate * sums[UNITS * i : UNITS * (i + 1)]).astype(BF16)
        sums = dot(turned[pl.ds(2 * UNITS, UNITS), :], cs[:, cols], ((1,), (0,))) * scale_hidden
        old = weights[pl.ds(2 * WIDE, UNITS), cols].astype(F32)
        new_buf[j, pl.ds(2 * UNITS, UNITS), :] = (old - learn_rate * sums).astype(BF16)
        if long:
            @pl.when(goes_long(j))
            def _():
                long_way(0, j).start()

            pl.when(jnp.logical_not(goes_long(j)))(lambda: gossip(j).start())
        else:
            gossip(j).start()

    chains = ((True, 0, 4), (True, 1, 3), (False, 0, 3), (False, 1, 4))

    def stop_place(n, m):
        onward = chains[n][2] - m
        return place_ahead(onward) if chains[n][0] else place_behind(onward)

    def chain_hop(n, m, src):
        return remote(src, chain.at[n, m], ch_ss.at[n, m], ch_rs.at[n, m], ahead if chains[n][0] else behind)

    def add_share(dst, src, place, pair):
        def some(i):
            at = pl.ds(pl.multiple_of(i * 16, 16), 16)
            rows = pl.ds(pl.multiple_of(place * PAIR + BLOCK * pair + i * 16, 16), 16)
            share = part[rows, mine] + part_sib[rows, :]
            dst[at, :] = (share if src is None else src(at) + share).astype(dst.dtype)

        loop(0, BLOCK // 16, some)

    def start_chains():
        for p in range(8):
            part_sibling(p).wait_recv()
        for n, (_, pair, _) in enumerate(chains):
            place = stop_place(n, 0)
            add_share(lead.at[n], None, place, pair)
            chain_hop(n, 0, lead.at[n]).start()

    def chain_step(m):
        for n, (_, pair, stops) in enumerate(chains):
            def go(n=n, pair=pair):
                at = chain.at[n, m - 1]
                chain_hop(n, m - 1, at).wait_recv()
                add_share(at, lambda i: at[i, :].astype(F32), stop_place(n, m), pair)
                chain_hop(n, m, at).start()

            if stops == 4:
                go()
            else:
                pl.when(m < stops)(go)

    def places(k, work):
        loop(jnp.maximum(2 * k - 1, 0), jnp.where(k < 0, 0, jnp.minimum(2 * k + 1, 8)), work)

    def step(k):
        @pl.when(k <= 4)
        def _():
            x_hop(True, k).wait_recv()

            @pl.when(k <= 3)
            def _():
                x_hop(True, k + 1).start()

            x_across(first_place(k)).start()

            @pl.when(k <= 3)
            def _():
                x_hop(False, k).wait_recv()

                @pl.when(k <= 2)
                def _():
                    x_hop(False, k + 1).start()

                x_across(second_place(k)).start()

        def from_across(place):
            x_across(place).wait_recv()
            x_sibling(place).start()

        def take_c(forward, pair):
            far = forward == (pair == 0)

            @pl.when(k <= (5 if far else 4))
            def _():
                @pl.when(k >= 2)
                def _():
                    c_hop(forward, k - 1, pair).wait_recv()

                @pl.when(jnp.logical_and(k <= (4 if far else 3), k >= (2 if pair == 0 else 1)))
                def _():
                    c_hop(forward, k, pair).start()

        places(k - 2, forward_b)
        places(k - 1, from_across)
        places(k - 2, turn_pair)

        @pl.when(k < 6)
        def _():
            places(k - 3, backward)

        take_c(True, 0)
        take_c(False, 0)
        places(k - 1, forward_a)

        @pl.when(k == 1)
        def _():
            c_across.wait_recv()

        take_c(False, 1)
        take_c(True, 1)
        places(k - 1, lambda place: c_sibling(place).start())

        @pl.when(k == 7)
        def _():
            loop(5, 8, backward)
            start_chains()

        @pl.when(k >= 8)
        def _():
            chain_step(k - 7)
            if long:
                pl.when(k == 8)(lambda: pass_on(1))

        done = jnp.where(k >= 8, early + 2 * (k - 8), 0)
        goal = jnp.where(k >= 8, jnp.minimum(done + 2, PIECES), jnp.where(k == 6, early, 0))
        loop(done, goal, update)

    loop(1, 11, step)

    for n in (1, 3):
        chain_hop(n, chains[n][2] - 1, chain.at[n, 0]).wait_recv()
    add_share(ysend, lambda i: chain[1, 2, i, :].astype(F32) + chain[3, 3, i, :].astype(F32), 0, 1)
    y_sum = remote(ysend, ybuf, ys_ss, ys_rs, across)
    y_sum.start()
    if long:
        pass_on(2)
    for n in (0, 2):
        chain_hop(n, chains[n][2] - 1, chain.at[n, 0]).wait_recv()
    add_share(fin, lambda i: chain[0, 3, i, :].astype(F32) + chain[2, 2, i, :].astype(F32), 0, 0)
    y_sum.wait_recv()
    fin[...] = (fin[...] + ybuf[...].astype(F32)) * scale_model
    theirs = pl.ds(pl.multiple_of((1 - c) * 40, 8), 40)
    rows_fly = remote(fin.at[theirs, :], rows32.at[:, mine], f_ss, f_rs, sibling)
    rows_fly.start()
    rows32[:, mine] = fin[forty, :]
    rows_fly.wait_recv()
    grad_out[0] = rows32[...].astype(BF16)

    for copy in (*pairs, c_across, y_sum, rows_fly):
        copy.wait_send()

    def sent(place):
        x_across(place).wait_send()
        x_sibling(place).wait_send()
        c_sibling(place).wait_send()
        part_sibling(place).wait_send()

    loop(0, 8, sent)

    def hops_sent(k):
        x_hop(True, k).wait_send()
        c_hop(True, k, 0).wait_send()
        c_hop(False, k, 1).wait_send()
        chain_hop(0, k - 1, chain.at[0, 0]).wait_send()
        chain_hop(3, k - 1, chain.at[0, 0]).wait_send()

        @pl.when(k <= 3)
        def _():
            x_hop(False, k).wait_send()
            c_hop(True, k, 1).wait_send()
            c_hop(False, k, 0).wait_send()
            chain_hop(1, k - 1, chain.at[0, 0]).wait_send()
            chain_hop(2, k - 1, chain.at[0, 0]).wait_send()

    loop(1, 5, hops_sent)

    def outs(j):
        cols = pl.ds(pl.multiple_of(j * PIECE, PIECE), PIECE)
        return [
            pltpu.make_async_copy(peer_buf.at[j, pl.ds(UNITS * i, UNITS), :], out.at[0, :, cols], out_sem.at[i])
            for i, out in enumerate((gate_out, up_out, down_out))
        ]

    def mean_step(i):
        j = lax.rem(i + long + 1, PIECES) if long else i
        gossip(j).wait_recv()

        def some(i):
            at = pl.ds(pl.multiple_of(i * 144, 16), 144)
            mean = (new_buf[j, at, :].astype(F32) + peer_buf[j, at, :].astype(F32)) * 0.5
            peer_buf[j, at, :] = mean.astype(BF16)

        loop(0, 3 * UNITS // 144, some)
        for copy in outs(j):
            copy.start()

    loop(0, PIECES, mean_step)

    def finish(j):
        if long:
            @pl.when(goes_long(j))
            def _():
                for hop_number in range(3):
                    long_way(hop_number, j).wait_send()

            pl.when(jnp.logical_not(goes_long(j)))(lambda: gossip(j).wait_send())
        else:
            gossip(j).wait_send()

    loop(0, PIECES, finish)
    for i, out in enumerate((gate_out, up_out, down_out)):
        pltpu.make_async_copy(out.at[0], out.at[0], out_sem.at[i]).wait()


def call(distance, arrays):
    dma = pltpu.SemaphoreType.DMA
    link = BF16 if distance == 2 else F32
    y_link = BF16 if distance == 1 else F32
    vmem = pl.BlockSpec(memory_space=pltpu.VMEM)
    hbm = pl.BlockSpec(memory_space=pl.ANY)
    return pl.pallas_call(
        functools.partial(kernel, distance),
        out_shape=(jax.ShapeDtypeStruct((1, 40, D), BF16),) + (jax.ShapeDtypeStruct((1, UNITS, D), BF16),) * 3,
        in_specs=[vmem, vmem, hbm, hbm, hbm],
        out_specs=(vmem, hbm, hbm, hbm),
        scratch_shapes=[
            pltpu.VMEM((TOKENS, D), BF16),
            pltpu.VMEM((TOKENS, D), BF16),
            pltpu.VMEM((3 * WIDE, D), BF16),
            pltpu.VMEM((TOKENS, 2 * WIDE), BF16),
            pltpu.VMEM((TOKENS, WIDE), BF16),
            pltpu.VMEM((3 * UNITS, TOKENS), BF16),
            pltpu.VMEM((4, PAIR, 2 * WIDE), F32),
            pltpu.VMEM((TOKENS, D), F32),
            pltpu.VMEM((TOKENS, HALF), F32),
            pltpu.VMEM((4, BLOCK, HALF), link),
            pltpu.VMEM((4, 4, BLOCK, HALF), link),
            pltpu.VMEM((PIECES, 3 * UNITS, PIECE), BF16),
            pltpu.VMEM((PIECES, 3 * UNITS, PIECE), BF16),
            pltpu.VMEM((2, LONG, 3 * UNITS, PIECE) if distance == 2 else (2, LONG, 16, 128), BF16),
            pltpu.VMEM((2, 40, D), F32),
            pltpu.VMEM((2, BLOCK, HALF), F32),
            pltpu.VMEM((BLOCK, HALF), y_link),
            pltpu.VMEM((BLOCK, HALF), y_link),
            pltpu.VMEM((BLOCK, HALF), F32),
            pltpu.VMEM((40, D), F32),
            dma((3,)), dma((2,)), dma((2,)),
            dma((16,)), dma((16,)), dma((16,)), dma((16,)), dma((8,)), dma((8,)), dma, dma,
            dma((8,)), dma((8,)), dma((8,)), dma((8,)), dma((8,)), dma((8,)), dma((4, 4)), dma((4, 4)),
            dma, dma, dma, dma,
            dma((PIECES,)), dma((PIECES,)), dma((3,)), dma((3, LONG)), dma((2, LONG)),
        ],
        compiler_params=pltpu.CompilerParams(
            collective_id=distance, has_side_effects=True, vmem_limit_bytes=63 * 2**20
        ),
        cost_estimate=pl.CostEstimate(flops=13600000000, bytes_accessed=10000000, transcendentals=400000),
        name=f"gossip_by_{distance}",
    )(*arrays)


def hand_over_kernel(*refs):
    sources, results, (held, in_sem, out_sem) = refs[:3], refs[3:6], refs[6:]
    spots = [(i, j, pl.ds(96 * j, 96)) for i in range(3) for j in range(3)]
    ins = [pltpu.make_async_copy(sources[i].at[0, at, :], held.at[i, at, :], in_sem.at[i, j]) for i, j, at in spots]
    outs = [pltpu.make_async_copy(held.at[i, at, :], results[i].at[0, at, :], out_sem.at[i, j]) for i, j, at in spots]
    for copy in ins:
        copy.start()
    for arrived, leaving in zip(ins, outs):
        arrived.wait()
        leaving.start()
    for copy in outs:
        copy.wait()


def hand_over(arrays):
    hbm = pl.BlockSpec(memory_space=pl.ANY)
    return pl.pallas_call(
        hand_over_kernel,
        out_shape=(jax.ShapeDtypeStruct((1, UNITS, D), BF16),) * 3,
        in_specs=[hbm] * 3,
        out_specs=(hbm,) * 3,
        scratch_shapes=[
            pltpu.VMEM((3, UNITS, D), BF16),
            pltpu.SemaphoreType.DMA((3, 3)),
            pltpu.SemaphoreType.DMA((3, 3)),
        ],
        compiler_params=pltpu.CompilerParams(vmem_limit_bytes=63 * 2**20),
        name="hand_over",
    )(*arrays)


def body(inputs, cotangent, gate_weight, up_weight, down_weight, step):
    arrays = (
        inputs, cotangent, jnp.swapaxes(gate_weight, 1, 2), jnp.swapaxes(up_weight, 1, 2), down_weight,
    )
    branches = [functools.partial(call, 1 << power) for power in range(3)]
    grad, *means = lax.switch(step[0] % 3, branches, arrays)
    gate, up, down = hand_over(means)
    return grad, jnp.swapaxes(gate, 1, 2), jnp.swapaxes(up, 1, 2), down


def solution(mesh):
    in_specs = (
        P("replica", "tensor", None),
        P("replica", "tensor", None),
        P("replica", None, "tensor"),
        P("replica", None, "tensor"),
        P("replica", "tensor", None),
        P(),
    )
    out_specs = (
        P("replica", "tensor", None),
        P("replica", None, "tensor"),
        P("replica", None, "tensor"),
        P("replica", "tensor", None),
    )
    return jax.shard_map(body, mesh=mesh, in_specs=in_specs, out_specs=out_specs, check_vma=False)
```

```python
import functools
import math

import jax
import jax.numpy as jnp
from jax import lax
from jax.experimental import pallas as pl
from jax.experimental.pallas import tpu as pltpu
from jax.sharding import PartitionSpec as P

D = 2304
FF = 9216
TOKENS = 1280
UNITS = 288
WIDE = 384
BLOCK = 80
PAIR = 160
HALF = D // 2
PIECE = 256
PIECES = D // PIECE
EARLY = 4
LONG = 2

gelu_c = 0.7978845608028654
gelu_k = 0.044715
learn_rate = 1.0
scale_model = 1.0 / math.sqrt(D)
scale_hidden = 1.0 / math.sqrt(FF)

MESH = pl.DeviceIdType.MESH
F32 = jnp.float32
BF16 = jnp.bfloat16


def gelu_parts(value):
    inner = gelu_c * (value + gelu_k * value * value * value)
    tangent = jnp.tanh(inner)
    act = 0.5 * value * (1.0 + tangent)
    slope = 0.5 * (1.0 + tangent) + 0.5 * value * (1.0 - tangent * tangent) * gelu_c * (
        1.0 + 3.0 * gelu_k * value * value
    )
    return act, slope


def dot(left, right, dims):
    return lax.dot_general(left, right, (dims, ((), ())), preferred_element_type=F32)


def place_behind(k):
    return jnp.maximum(2 * k - 1, 0)


def place_ahead(k):
    return jnp.minimum(2 * k, 7)


def block_rows(place, pair):
    return pl.ds(pl.multiple_of(place * PAIR + BLOCK * pair, 16), BLOCK)


def pair_rows(place):
    return pl.ds(pl.multiple_of(place * PAIR, 16), PAIR)


def loop(first, end, step):
    def one(i, carry):
        step(i)
        return carry

    lax.fori_loop(first, end, one, 0)


def kernel(
    distance,
    x_in, cot_in, wg_in, wu_in, wd_in,
    grad_out, gate_out, up_out, down_out,
    xs, cs, weights, gu, hid, turned, gate_up, part, part_sib, lead, chain, new_buf, peer_buf, relay,
    wide32, pair32, ysend, ybuf, fin, rows32,
    load_sem, pair_ss, pair_rs, zx_ss, zx_rs, zc_ss, zc_rs, yx_ss, yx_rs, yc_ss, yc_rs,
    sx_ss, sx_rs, sc_ss, sc_rs, p_ss, p_rs, ch_ss, ch_rs, ys_ss, ys_rs, f_ss, f_rs,
    g_ss, g_rs, out_sem, r_ss, r_rs,
):
    r = lax.axis_index("replica")
    t = lax.axis_index("tensor")
    z, yh, c = t // 4, (t // 2) % 2, t % 2
    base = yh * 2 + c
    ahead = (r, lax.rem(z + 1, 8) * 4 + base)
    behind = (r, lax.rem(z + 7, 8) * 4 + base)
    across = (r, z * 4 + (1 - yh) * 2 + c)
    sibling = (r, z * 4 + yh * 2 + (1 - c))
    gives_to = (lax.rem(r + 8 - distance, 8), t)
    takes_from = (lax.rem(r + distance, 8), t)

    long = LONG if distance == 2 else 0
    early = EARLY + (1 if long else 0)
    onward = (r, lax.rem(z + 1 + 6 * c, 8) * 4 + base)
    backward_on = (r, lax.rem(z + 7 - 6 * c, 8) * 4 + base)

    mine = pl.ds(pl.multiple_of(c * HALF, 128), HALF)
    other = pl.ds(pl.multiple_of((1 - c) * HALF, 128), HALF)

    def remote(src, dst, ss, rs, device):
        return pltpu.make_async_remote_copy(
            src_ref=src, dst_ref=dst, send_sem=ss, recv_sem=rs, device_id=device, device_id_type=MESH
        )

    loads = [
        pltpu.make_async_copy(source.at[0], weights.at[pl.ds(WIDE * i, UNITS), :], load_sem.at[i])
        for i, source in enumerate((wg_in, wu_in, wd_in))
    ]
    for load in loads:
        load.start()

    barrier = pltpu.get_barrier_semaphore()
    senders = (ahead, behind, across, sibling, takes_from) + ((gives_to,) if long else ())
    for device in senders:
        pl.semaphore_signal(barrier, inc=1, device_id=device, device_id_type=MESH)
    wide32[0] = x_in[0].astype(F32)
    wide32[1] = cot_in[0].astype(F32)
    pl.semaphore_wait(barrier, len(senders))

    forty = pl.ds(pl.multiple_of(c * 40, 8), 40)
    pairs = [
        remote(wide32.at[a, :, other], pair32.at[a, forty, :], pair_ss.at[a], pair_rs.at[a], sibling) for a in range(2)
    ]
    for copy in pairs:
        copy.start()
    for a in range(2):
        pair32[a, forty, :] = wide32[a, :, mine]

    def first_place(k):
        return jnp.where(c == 0, place_behind(k), place_ahead(k))

    def second_place(k):
        return jnp.where(c == 0, place_ahead(k), place_behind(k))

    def hop(buf, ss, rs, forward, k, pair):
        place = first_place if forward else second_place
        slot = 2 * place(k) + pair
        return remote(
            buf.at[block_rows(place(k - 1), pair), mine], buf.at[block_rows(place(k), pair), mine],
            ss.at[slot], rs.at[slot], onward if forward else backward_on,
        )

    def x_hop(forward, k):
        return hop(xs, zx_ss, zx_rs, forward, k, 0)

    def c_hop(forward, k, pair):
        return hop(cs, zc_ss, zc_rs, forward, k, pair)

    def x_across(place):
        return remote(
            xs.at[block_rows(place, 0), mine], xs.at[block_rows(place, 1), mine],
            yx_ss.at[place], yx_rs.at[place], across,
        )

    c_across = remote(cs.at[block_rows(0, 0), mine], cs.at[block_rows(0, 1), mine], yc_ss, yc_rs, across)

    def x_sibling(place):
        at = xs.at[pair_rows(place), mine]
        return remote(at, at, sx_ss.at[place], sx_rs.at[place], sibling)

    def c_sibling(place):
        at = cs.at[pair_rows(place), mine]
        return remote(at, at, sc_ss.at[place], sc_rs.at[place], sibling)

    def part_sibling(place):
        rows = pair_rows(place)
        return remote(part.at[rows, other], part_sib.at[rows, :], p_ss.at[place], p_rs.at[place], sibling)

    pairs[0].wait_recv()
    xs[pl.ds(0, BLOCK), mine] = pair32[0].astype(BF16)
    x_hop(True, 1).start()
    x_hop(False, 1).start()
    x_across(0).start()
    pairs[1].wait_recv()
    cs[pl.ds(0, BLOCK), mine] = pair32[1].astype(BF16)
    c_across.start()

    for i in range(3):
        weights[pl.ds(WIDE * i + UNITS, WIDE - UNITS), :] = jnp.zeros((WIDE - UNITS, D), BF16)
    for forward in (True, False):
        c_hop(forward, 1, 0).start()
    for load in loads:
        load.wait()

    def forward_a(place):
        x_sibling(place).wait_recv()
        gate_up[lax.rem(place, 4)] = dot(xs[pair_rows(place), :], weights[pl.ds(0, 2 * WIDE), :], ((1,), (1,)))

    def forward_b(place):
        c_sibling(place).wait_recv()
        at = lax.rem(place, 4)
        rows = pair_rows(place)
        hidden_grad = dot(cs[rows, :], weights[pl.ds(2 * WIDE, WIDE), :], ((1,), (1,))) * scale_hidden
        gate = gate_up[at, :, pl.ds(0, WIDE)] * scale_model
        up = gate_up[at, :, pl.ds(WIDE, WIDE)] * scale_model
        act, slope = gelu_parts(gate)
        hid[rows, :] = (act * up).astype(BF16)
        gu[rows, pl.ds(0, WIDE)] = (hidden_grad * up * slope).astype(BF16)
        gu[rows, pl.ds(WIDE, WIDE)] = (hidden_grad * act).astype(BF16)

    def turn(b):
        rows = pl.ds(pl.multiple_of(b * 128, 128), 128)
        turned[pl.ds(0, UNITS), rows] = gu[rows, pl.ds(0, WIDE)].T[0:UNITS]
        turned[pl.ds(UNITS, UNITS), rows] = gu[rows, pl.ds(WIDE, WIDE)].T[0:UNITS]
        turned[pl.ds(2 * UNITS, UNITS), rows] = hid[rows, :].T[0:UNITS]

    def turn_pair(place):
        loop((PAIR * place) // 128, (PAIR * (place + 1)) // 128, turn)

    def backward(place):
        rows = pair_rows(place)

        def columns(j):
            cols = pl.ds(pl.multiple_of(j * 768, 768), 768)
            part[rows, cols] = dot(gu[rows, :], weights[pl.ds(0, 2 * WIDE), cols], ((1,), (0,)))

        loop(0, 3, columns)
        part_sibling(place).start()

    def gossip(j):
        return remote(new_buf.at[j], peer_buf.at[j], g_ss.at[j], g_rs.at[j], gives_to)

    def goes_long(j):
        return jnp.logical_and(j >= 1, j <= long)

    def long_way(hop_number, j):
        src = new_buf.at[j] if hop_number == 0 else relay.at[hop_number - 1, j - 1]
        if hop_number == 2:
            return remote(src, peer_buf.at[j], r_ss.at[2, j - 1], g_rs.at[j], takes_from)
        return remote(
            src, relay.at[hop_number, j - 1], r_ss.at[hop_number, j - 1], r_rs.at[hop_number, j - 1], takes_from
        )

    def pass_on(hop_number):
        def one(j):
            long_way(hop_number - 1, j).wait_recv()
            long_way(hop_number, j).start()

        loop(1, long + 1, one)

    def update(j):
        cols = pl.ds(pl.multiple_of(j * PIECE, PIECE), PIECE)
        sums = dot(turned[pl.ds(0, 2 * UNITS), :], xs[:, cols], ((1,), (0,))) * scale_model
        for i in range(2):
            old = weights[pl.ds(WIDE * i, UNITS), cols].astype(F32)
            new_buf[j, pl.ds(UNITS * i, UNITS), :] = (old - learn_rate * sums[UNITS * i : UNITS * (i + 1)]).astype(BF16)
        sums = dot(turned[pl.ds(2 * UNITS, UNITS), :], cs[:, cols], ((1,), (0,))) * scale_hidden
        old = weights[pl.ds(2 * WIDE, UNITS), cols].astype(F32)
        new_buf[j, pl.ds(2 * UNITS, UNITS), :] = (old - learn_rate * sums).astype(BF16)
        if long:
            @pl.when(goes_long(j))
            def _():
                long_way(0, j).start()

            pl.when(jnp.logical_not(goes_long(j)))(lambda: gossip(j).start())
        else:
            gossip(j).start()

    chains = ((True, 0, 4), (True, 1, 3), (False, 0, 3), (False, 1, 4))

    def stop_place(n, m):
        onward = chains[n][2] - m
        return place_ahead(onward) if chains[n][0] else place_behind(onward)

    def chain_hop(n, m, src):
        return remote(src, chain.at[n, m], ch_ss.at[n, m], ch_rs.at[n, m], ahead if chains[n][0] else behind)

    def add_share(dst, src, place, pair):
        def some(i):
            at = pl.ds(pl.multiple_of(i * 16, 16), 16)
            rows = pl.ds(pl.multiple_of(place * PAIR + BLOCK * pair + i * 16, 16), 16)
            share = part[rows, mine] + part_sib[rows, :]
            dst[at, :] = (share if src is None else src(at) + share).astype(dst.dtype)

        loop(0, BLOCK // 16, some)

    def start_chains():
        for p in range(8):
            part_sibling(p).wait_recv()
        for n, (_, pair, _) in enumerate(chains):
            place = stop_place(n, 0)
            add_share(lead.at[n], None, place, pair)
            chain_hop(n, 0, lead.at[n]).start()

    def chain_step(m):
        for n, (_, pair, stops) in enumerate(chains):
            def go(n=n, pair=pair):
                at = chain.at[n, m - 1]
                chain_hop(n, m - 1, at).wait_recv()
                add_share(at, lambda i: at[i, :].astype(F32), stop_place(n, m), pair)
                chain_hop(n, m, at).start()

            if stops == 4:
                go()
            else:
                pl.when(m < stops)(go)

    def places(k, work):
        loop(jnp.maximum(2 * k - 1, 0), jnp.where(k < 0, 0, jnp.minimum(2 * k + 1, 8)), work)

    def step(k):
        @pl.when(k <= 4)
        def _():
            x_hop(True, k).wait_recv()

            @pl.when(k <= 3)
            def _():
                x_hop(True, k + 1).start()

            x_across(first_place(k)).start()

            @pl.when(k <= 3)
            def _():
                x_hop(False, k).wait_recv()

                @pl.when(k <= 2)
                def _():
                    x_hop(False, k + 1).start()

                x_across(second_place(k)).start()

        def from_across(place):
            x_across(place).wait_recv()
            x_sibling(place).start()

        def take_c(forward, pair):
            far = forward == (pair == 0)

            @pl.when(k <= (5 if far else 4))
            def _():
                @pl.when(k >= 2)
                def _():
                    c_hop(forward, k - 1, pair).wait_recv()

                @pl.when(jnp.logical_and(k <= (4 if far else 3), k >= (2 if pair == 0 else 1)))
                def _():
                    c_hop(forward, k, pair).start()

        places(k - 2, forward_b)
        places(k - 1, from_across)
        places(k - 2, turn_pair)

        @pl.when(k < 6)
        def _():
            places(k - 3, backward)

        take_c(True, 0)
        take_c(False, 0)
        places(k - 1, forward_a)

        @pl.when(k == 1)
        def _():
            c_across.wait_recv()

        take_c(False, 1)
        take_c(True, 1)
        places(k - 1, lambda place: c_sibling(place).start())

        @pl.when(k == 7)
        def _():
            loop(5, 8, backward)
            start_chains()

        @pl.when(k >= 8)
        def _():
            chain_step(k - 7)
            if long:
                pl.when(k == 8)(lambda: pass_on(1))

        done = jnp.where(k >= 8, early + 2 * (k - 8), 0)
        goal = jnp.where(k >= 8, jnp.minimum(done + 2, PIECES), jnp.where(k == 6, early, 0))
        loop(done, goal, update)

    loop(1, 11, step)

    for n in (1, 3):
        chain_hop(n, chains[n][2] - 1, chain.at[n, 0]).wait_recv()
    add_share(ysend, lambda i: chain[1, 2, i, :].astype(F32) + chain[3, 3, i, :].astype(F32), 0, 1)
    y_sum = remote(ysend, ybuf, ys_ss, ys_rs, across)
    y_sum.start()
    if long:
        pass_on(2)
    for n in (0, 2):
        chain_hop(n, chains[n][2] - 1, chain.at[n, 0]).wait_recv()
    add_share(fin, lambda i: chain[0, 3, i, :].astype(F32) + chain[2, 2, i, :].astype(F32), 0, 0)
    y_sum.wait_recv()
    fin[...] = (fin[...] + ybuf[...].astype(F32)) * scale_model
    theirs = pl.ds(pl.multiple_of((1 - c) * 40, 8), 40)
    rows_fly = remote(fin.at[theirs, :], rows32.at[:, mine], f_ss, f_rs, sibling)
    rows_fly.start()
    rows32[:, mine] = fin[forty, :]
    rows_fly.wait_recv()
    grad_out[0] = rows32[...].astype(BF16)

    for copy in (*pairs, c_across, y_sum, rows_fly):
        copy.wait_send()

    def sent(place):
        x_across(place).wait_send()
        x_sibling(place).wait_send()
        c_sibling(place).wait_send()
        part_sibling(place).wait_send()

    loop(0, 8, sent)

    def hops_sent(k):
        x_hop(True, k).wait_send()
        c_hop(True, k, 0).wait_send()
        c_hop(False, k, 1).wait_send()
        chain_hop(0, k - 1, chain.at[0, 0]).wait_send()
        chain_hop(3, k - 1, chain.at[0, 0]).wait_send()

        @pl.when(k <= 3)
        def _():
            x_hop(False, k).wait_send()
            c_hop(True, k, 1).wait_send()
            c_hop(False, k, 0).wait_send()
            chain_hop(1, k - 1, chain.at[0, 0]).wait_send()
            chain_hop(2, k - 1, chain.at[0, 0]).wait_send()

    loop(1, 5, hops_sent)

    def outs(j):
        cols = pl.ds(pl.multiple_of(j * PIECE, PIECE), PIECE)
        return [
            pltpu.make_async_copy(peer_buf.at[j, pl.ds(UNITS * i, UNITS), :], out.at[0, :, cols], out_sem.at[i])
            for i, out in enumerate((gate_out, up_out, down_out))
        ]

    def mean_step(i):
        j = lax.rem(i + long + 1, PIECES) if long else i
        gossip(j).wait_recv()

        def some(i):
            at = pl.ds(pl.multiple_of(i * 144, 16), 144)
            mean = (new_buf[j, at, :].astype(F32) + peer_buf[j, at, :].astype(F32)) * 0.5
            peer_buf[j, at, :] = mean.astype(BF16)

        loop(0, 3 * UNITS // 144, some)
        for copy in outs(j):
            copy.start()

    loop(0, PIECES, mean_step)

    def finish(j):
        if long:
            @pl.when(goes_long(j))
            def _():
                for hop_number in range(3):
                    long_way(hop_number, j).wait_send()

            pl.when(jnp.logical_not(goes_long(j)))(lambda: gossip(j).wait_send())
        else:
            gossip(j).wait_send()

    loop(0, PIECES, finish)
    for i, out in enumerate((gate_out, up_out, down_out)):
        pltpu.make_async_copy(out.at[0], out.at[0], out_sem.at[i]).wait()


def call(distance, arrays):
    dma = pltpu.SemaphoreType.DMA
    link = BF16 if distance == 2 else F32
    y_link = BF16 if distance == 1 else F32
    vmem = pl.BlockSpec(memory_space=pltpu.VMEM)
    hbm = pl.BlockSpec(memory_space=pl.ANY)
    return pl.pallas_call(
        functools.partial(kernel, distance),
        out_shape=(jax.ShapeDtypeStruct((1, 40, D), BF16),) + (jax.ShapeDtypeStruct((1, UNITS, D), BF16),) * 3,
        in_specs=[vmem, vmem, hbm, hbm, hbm],
        out_specs=(vmem, hbm, hbm, hbm),
        scratch_shapes=[
            pltpu.VMEM((TOKENS, D), BF16),
            pltpu.VMEM((TOKENS, D), BF16),
            pltpu.VMEM((3 * WIDE, D), BF16),
            pltpu.VMEM((TOKENS, 2 * WIDE), BF16),
            pltpu.VMEM((TOKENS, WIDE), BF16),
            pltpu.VMEM((3 * UNITS, TOKENS), BF16),
            pltpu.VMEM((4, PAIR, 2 * WIDE), F32),
            pltpu.VMEM((TOKENS, D), F32),
            pltpu.VMEM((TOKENS, HALF), F32),
            pltpu.VMEM((4, BLOCK, HALF), link),
            pltpu.VMEM((4, 4, BLOCK, HALF), link),
            pltpu.VMEM((PIECES, 3 * UNITS, PIECE), BF16),
            pltpu.VMEM((PIECES, 3 * UNITS, PIECE), BF16),
            pltpu.VMEM((2, LONG, 3 * UNITS, PIECE) if distance == 2 else (2, LONG, 16, 128), BF16),
            pltpu.VMEM((2, 40, D), F32),
            pltpu.VMEM((2, BLOCK, HALF), F32),
            pltpu.VMEM((BLOCK, HALF), y_link),
            pltpu.VMEM((BLOCK, HALF), y_link),
            pltpu.VMEM((BLOCK, HALF), F32),
            pltpu.VMEM((40, D), F32),
            dma((3,)), dma((2,)), dma((2,)),
            dma((16,)), dma((16,)), dma((16,)), dma((16,)), dma((8,)), dma((8,)), dma, dma,
            dma((8,)), dma((8,)), dma((8,)), dma((8,)), dma((8,)), dma((8,)), dma((4, 4)), dma((4, 4)),
            dma, dma, dma, dma,
            dma((PIECES,)), dma((PIECES,)), dma((3,)), dma((3, LONG)), dma((2, LONG)),
        ],
        compiler_params=pltpu.CompilerParams(
            collective_id=distance, has_side_effects=True, vmem_limit_bytes=63 * 2**20
        ),
        cost_estimate=pl.CostEstimate(flops=13600000000, bytes_accessed=10000000, transcendentals=400000),
        name=f"gossip_by_{distance}",
    )(*arrays)


def hand_over_kernel(*refs):
    grad_in, sources, grad, results = refs[0], refs[1:4], refs[4], refs[5:8]
    held, in_sem, out_sem, grad_sem = refs[8:]
    grad_copy = pltpu.make_async_copy(grad_in, grad, grad_sem)
    grad_copy.start()
    spots = [(i, j, pl.ds(96 * j, 96)) for i in range(3) for j in range(3)]
    ins = [pltpu.make_async_copy(sources[i].at[0, at, :], held.at[i, at, :], in_sem.at[i, j]) for i, j, at in spots]
    outs = [pltpu.make_async_copy(held.at[i, at, :], results[i].at[0, at, :], out_sem.at[i, j]) for i, j, at in spots]
    for copy in ins:
        copy.start()
    for arrived, leaving in zip(ins, outs):
        arrived.wait()
        leaving.start()
    for copy in outs:
        copy.wait()
    grad_copy.wait()


def hand_over(arrays):
    hbm = pl.BlockSpec(memory_space=pl.ANY)
    return pl.pallas_call(
        hand_over_kernel,
        out_shape=(jax.ShapeDtypeStruct((1, 40, D), BF16),) + (jax.ShapeDtypeStruct((1, UNITS, D), BF16),) * 3,
        in_specs=[pl.BlockSpec(memory_space=pltpu.VMEM)] + [hbm] * 3,
        out_specs=(hbm,) * 4,
        scratch_shapes=[
            pltpu.VMEM((3, UNITS, D), BF16),
            pltpu.SemaphoreType.DMA((3, 3)),
            pltpu.SemaphoreType.DMA((3, 3)),
            pltpu.SemaphoreType.DMA,
        ],
        compiler_params=pltpu.CompilerParams(vmem_limit_bytes=63 * 2**20),
        name="hand_over",
    )(*arrays)


def body(inputs, cotangent, gate_weight, up_weight, down_weight, step):
    arrays = (
        inputs, cotangent, jnp.swapaxes(gate_weight, 1, 2), jnp.swapaxes(up_weight, 1, 2), down_weight,
    )
    branches = [functools.partial(call, 1 << power) for power in range(3)]
    grad, gate, up, down = hand_over(lax.switch(step[0] % 3, branches, arrays))
    return grad, jnp.swapaxes(gate, 1, 2), jnp.swapaxes(up, 1, 2), down


def solution(mesh):
    in_specs = (
        P("replica", "tensor", None),
        P("replica", "tensor", None),
        P("replica", None, "tensor"),
        P("replica", None, "tensor"),
        P("replica", "tensor", None),
        P(),
    )
    out_specs = (
        P("replica", "tensor", None),
        P("replica", None, "tensor"),
        P("replica", None, "tensor"),
        P("replica", "tensor", None),
    )
    return jax.shard_map(body, mesh=mesh, in_specs=in_specs, out_specs=out_specs, check_vma=False)
```
